512 devices in a mesh: tm: 256 (over z, y, x), mp: 2 (over core).
Axes of the slice: x: 4, y: 8, z: 8, core: 2. Of those that a mesh axis runs over, the one named last changes fastest.
Arguments:
- frames: bfloat16 [131072, 1024], P('tm'), may hold values from -6 to 6
- gain_attn: float32 [1024], replicated, may hold values from 0.5 to 1.5
- w_qkv: bfloat16 [1024, 3, 1024], P(None, None, 'mp'), may hold values from -1 to 1
- w_out: bfloat16 [1024, 1024], P('mp'), may hold values from -0.1875 to 0.1875
- gain_conv: float32 [1024], replicated, may hold values from 0.5 to 1.5
- w_point_in: bfloat16 [1024, 2048], replicated, may hold values from -0.1875 to 0.1875
- w_depth: bfloat16 [31, 1024], replicated, may hold values from -1 to 1
- gain_depth: float32 [1024], replicated, may hold values from 0.5 to 1.5
- w_point_out: bfloat16 [1024, 1024], replicated, may hold values from -0.1875 to 0.1875
- gain_ffn: float32 [1024], replicated, may hold values from 0.5 to 1.5
- w_up: bfloat16 [1024, 4096], P(None, 'mp'), may hold values from -0.1875 to 0.1875
- w_down: bfloat16 [4096, 1024], P('mp'), may hold values from -0.09375 to 0.09375
- gain_final: float32 [1024], replicated, may hold values from 0.5 to 1.5
- lengths: int32 [128], replicated, may hold values from 1 to 16, 1024 in all
- context: int32 [128], replicated, may hold values from 0 to 8, as said below
Outputs:
- encoded: bfloat16 [131072, 1024], P(('tm', 'mp'))
The draws below stay inside these ranges and needn't reach their ends.
Inputs may be any that keep to these rules, and one draw needn't show every extreme that they name: Recording lengths in stretches of 128 frames; the recordings fill all 131072 frames in order, and the longest has exactly 16 stretches. `context`: some recording allows exactly 8 stretches.
All inputs are finite; a program needn't handle non-finite values.
Results may differ from the reference program's by a relative error of at most 0.014.
The reference program's roundings to bfloat16 on the way count: a program that leaves them out, or rounds other values in their place, can miss the bound.
Values may be sent and summed in bfloat16 or wider, within the bound.
No kernel may reach another device: no remote copies, remote signals or barrier semaphores. Data moves between devices by JAX's collectives and lax.ppermute only.
A program may use at most 192 MiB of HBM per device.

```python
import math
import jax
import jax.numpy as jnp
import numpy as np
from jax import lax

D = 1024
H = 16
HD = 64
FF = 4096
KER = 31
S = 512
C = 128
LMAX = 8
NREC = 128
TOTAL = 131072
N_MP = 2


def draw_w_qkv(key, part):
    key = jax.random.fold_in(key, 11)
    base = jax.random.normal(key, (D, 3, D), jnp.float32) * D ** (-0.5)
    return base.astype(jnp.bfloat16)


def draw_context(key, part):
    key = jax.random.fold_in(key, 7)
    first_key, second_key = jax.random.split(key)
    drawn = jax.random.randint(first_key, (NREC,), 0, LMAX + 1)
    chosen = jax.random.randint(second_key, (), 0, NREC)
    return jnp.where(jnp.arange(NREC) == chosen, LMAX, drawn).astype(jnp.int32)


def block_levels(rng, dims, pieces, smallest, high):
    level = 1.0
    for position, parts in pieces:
        heights = jax.random.uniform(jax.random.fold_in(jax.random.fold_in(rng, 6), position), (parts,), jnp.float32, smallest / len(pieces), high / len(pieces))
        level = level * jnp.repeat(jnp.exp(heights), dims[position] // parts).reshape((-1,) + (1,) * (len(dims) - 1 - position))
    return level


def split_up(number_of, total, most, skew):
    loads = [(1 << 20) // math.isqrt(rank ** skew) + 1 for rank in range(2, number_of + 1)]
    rest, counts = total - most - (number_of - 1), [1] * (number_of - 1)
    while rest > 0:
        free = [i for i in range(number_of - 1) if counts[i] < most]
        whole, left = sum([loads[i] for i in free]), rest
        for i in free:
            addition = min(most - counts[i], max(1, left * loads[i] // whole), rest)
            counts[i] = counts[i] + addition
            rest = rest - addition
    return np.array([most] + counts)


def ragged_sizes(stream_key, count, total, limit, lean):
    if count == 2:
        one = jax.random.randint(stream_key, (), max(1, total - limit), min(limit, total - 1) + 1)
        return jnp.stack([one, total - one])
    sizes = jnp.asarray(split_up(count, total, limit, lean), jnp.int32)
    pairs = (count - 1) // 2
    source_of, receiver = sizes[1:1 + 2 * pairs:2], sizes[2:2 + 2 * pairs:2]
    margin = jnp.minimum(source_of - 1, limit - receiver)
    passed = jax.random.randint(jax.random.fold_in(stream_key, 1), (pairs,), 0, 1 << 20) % (margin + 1)
    sizes = sizes.at[1:1 + 2 * pairs:2].set(source_of - passed).at[2:2 + 2 * pairs:2].set(receiver + passed)
    return sizes[jax.random.permutation(jax.random.fold_in(stream_key, 2), count)]


def bell_draw(key, shape, scale, bound, pieces=(), kind=jnp.bfloat16):
    entries = jax.random.normal(key, shape, jnp.float32) * scale
    if len(pieces) > 0:
        entries = block_levels(key, shape, pieces, -0.22, 0.18) * entries
    return jnp.clip(entries, min=-bound, max=bound).astype(kind)


def setup_inputs(seed: int = 0) -> dict:
    key_of = jax.random.split(jax.random.key(seed), 16)
    return {
        "frames": bell_draw(key_of[0], (TOTAL, D), 1.0, 6.0, ((0, 256),)),
        "gain_attn": jnp.clip(1.0 + 0.1 * jax.random.normal(key_of[1], (D,), jnp.float32), 0.5, 1.5),
        "w_qkv": draw_w_qkv(jax.random.fold_in(key_of[15], 71), 0),
        "w_out": bell_draw(key_of[3], (D, D), D ** -0.5, 0.1875, ((0, 2),)),
        "gain_conv": jnp.clip(1.0 + 0.1 * jax.random.normal(key_of[4], (D,), jnp.float32), 0.5, 1.5),
        "w_point_in": bell_draw(key_of[5], (D, 2 * D), D ** -0.5, 0.1875),
        "w_depth": bell_draw(key_of[6], (KER, D), KER ** -0.5, 1.0),
        "gain_depth": jnp.clip(1.0 + 0.1 * jax.random.normal(key_of[7], (D,), jnp.float32), 0.5, 1.5),
        "w_point_out": bell_draw(key_of[8], (D, D), D ** -0.5, 0.1875),
        "gain_ffn": jnp.clip(1.0 + 0.1 * jax.random.normal(key_of[9], (D,), jnp.float32), 0.5, 1.5),
        "w_up": bell_draw(key_of[10], (D, FF), D ** -0.5, 0.1875, ((1, 2),)),
        "w_down": bell_draw(key_of[11], (FF, D), FF ** -0.5, 0.09375, ((0, 2),)),
        "gain_final": jnp.clip(1.0 + 0.1 * jax.random.normal(key_of[12], (D,), jnp.float32), 0.5, 1.5),
        "lengths": ragged_sizes(key_of[13], NREC, TOTAL // C, 4 * S // C, 0).astype(jnp.int32),
        "context": draw_context(jax.random.fold_in(key_of[15], 71), 0),
    }


EPSILON = 1e-05
NEGATIVE = -1e+30

def layer_norm(values, gain_vec):
    values = values.astype(jnp.float32)
    centred = values - lax.optimization_barrier(jnp.mean(values, axis=-1, keepdims=True))
    variance = lax.optimization_barrier(jnp.mean(centred * centred, axis=-1, keepdims=True))
    return centred * lax.rsqrt(variance + EPSILON) * gain_vec.astype(jnp.float32)

def lowest_stretches(stretch_start, stretch_end, context, stretch_count):
    stretch_ids = jnp.arange(stretch_count, dtype=jnp.int32)
    member = ((stretch_start[None, :] <= stretch_ids[:, None]) & (stretch_ids[:, None] < stretch_end[None, :])).astype(jnp.int32)
    opening = lax.optimization_barrier(jnp.sum(member * stretch_start[None, :], axis=1))
    reached = lax.optimization_barrier(jnp.sum(member * context[None, :], axis=1))
    return jnp.maximum(stretch_ids - reached, opening).astype(jnp.int32)

def record_labels(frame_ids, stretch_start, stretch_end):
    stretch_ids = jnp.floor_divide(frame_ids, C)
    member = ((stretch_start[None, :] <= stretch_ids[:, None]) & (stretch_ids[:, None] < stretch_end[None, :])).astype(jnp.int32)
    numbers = jnp.arange(1, stretch_start.shape[0] + 1, dtype=jnp.int32)
    return lax.optimization_barrier(jnp.sum(member * numbers[None, :], axis=1))

def softmax_weights(scores):
    highest = lax.optimization_barrier(jnp.max(scores, axis=-1, keepdims=True))
    raised = jnp.exp(scores - highest)
    return (raised / lax.optimization_barrier(jnp.sum(raised, axis=-1, keepdims=True))).astype(jnp.bfloat16)

def reference(frames, gain_attn, w_qkv, w_out, gain_conv, w_point_in, w_depth, gain_depth, w_point_out, gain_ffn, w_up, w_down, gain_final, lengths, context):
    frame_total = frames.shape[0]
    q_block = min(S, 512)
    key_span = 2 * S
    stretch_start = (jnp.cumsum(lengths) - lengths).astype(jnp.int32)
    stretch_end = (stretch_start + lengths).astype(jnp.int32)
    lowest = lowest_stretches(stretch_start, stretch_end, context, frame_total // C)
    normed = layer_norm(frames, gain_attn).astype(jnp.bfloat16)
    projected = jnp.dot(normed, w_qkv.reshape(D, 3 * D), preferred_element_type=jnp.float32).astype(jnp.bfloat16)
    queries = projected[:, :D]
    padding = jnp.zeros((key_span, D), jnp.bfloat16)
    keys_all = jnp.concatenate([padding, projected[:, D:2 * D]], axis=0)
    values_all = jnp.concatenate([padding, projected[:, 2 * D:]], axis=0)

    def attend(block_id):
        offset = (block_id * q_block).astype(jnp.int32)
        q_rows = lax.dynamic_slice_in_dim(queries, offset, q_block, 0).astype(jnp.float32).reshape(q_block, H, HD)
        k_rows = lax.dynamic_slice_in_dim(keys_all, offset, key_span + q_block, 0).astype(jnp.float32).reshape(key_span + q_block, H, HD)
        v_rows = lax.dynamic_slice_in_dim(values_all, offset, key_span + q_block, 0).astype(jnp.float32).reshape(key_span + q_block, H, HD)
        q_stretches = (offset + jnp.arange(q_block, dtype=jnp.int32)) // C
        low_rows = jnp.take(lowest, q_stretches)
        k_stretches = jnp.floor_divide(offset - key_span + jnp.arange(key_span + q_block, dtype=jnp.int32), C)
        visible = (k_stretches[None, :] >= low_rows[:, None]) & (k_stretches[None, :] <= q_stretches[:, None])
        scores = jnp.einsum('qhd,khd->hqk', q_rows, k_rows) * HD ** (-0.5)
        weights = softmax_weights(jnp.where(visible[None], scores, NEGATIVE))
        mixed_out = jnp.einsum('hqk,khd->qhd', weights.astype(jnp.float32), v_rows)
        return mixed_out.astype(jnp.bfloat16).reshape(q_block, D)
    heads_out = lax.map(attend, jnp.arange(frame_total // q_block, dtype=jnp.int32)).reshape(frame_total, D)
    group_width = D // N_MP
    attention = jnp.zeros((frame_total, D), jnp.float32)
    for member_id in range(N_MP):
        col_range = slice(member_id * group_width, (member_id + 1) * group_width)
        partial_out = jnp.dot(heads_out[:, col_range], w_out[col_range, :], preferred_element_type=jnp.float32)
        attention = attention + lax.optimization_barrier(partial_out.astype(jnp.bfloat16)).astype(jnp.float32)
    first_res = frames.astype(jnp.float32) + attention
    conv_in = layer_norm(first_res, gain_conv).astype(jnp.bfloat16)
    lifted = jnp.dot(conv_in, w_point_in, preferred_element_type=jnp.float32)
    gated_units = (lifted[:, :D] * jax.nn.sigmoid(lifted[:, D:])).astype(jnp.bfloat16)
    half_width = (KER - 1) // 2
    padded = jnp.pad(gated_units, ((half_width, half_width), (0, 0)))
    labels = record_labels(jnp.arange(-half_width, frame_total + half_width, dtype=jnp.int32), stretch_start, stretch_end)
    centre = labels[half_width:half_width + frame_total]
    tap_weights = w_depth.astype(jnp.float32)
    depth_sum = jnp.zeros((frame_total, D), jnp.float32)
    for offset in range(KER):
        same_record = (labels[offset:offset + frame_total] == centre)[:, None]
        depth_sum = depth_sum + jnp.where(same_record, padded[offset:offset + frame_total].astype(jnp.float32) * tap_weights[offset], 0.0)
    squashed = jax.nn.silu(layer_norm(depth_sum, gain_depth)).astype(jnp.bfloat16)
    second_res = first_res + jnp.dot(squashed, w_point_out, preferred_element_type=jnp.float32)
    ffn_in = layer_norm(second_res, gain_ffn).astype(jnp.bfloat16)
    hidden_width = FF // N_MP
    feed_sum = jnp.zeros((frame_total, D), jnp.float32)
    for member_id in range(N_MP):
        col_range = slice(member_id * hidden_width, (member_id + 1) * hidden_width)
        hidden = jax.nn.silu(jnp.dot(ffn_in, w_up[:, col_range], preferred_element_type=jnp.float32)).astype(jnp.bfloat16)
        partial_out = jnp.dot(hidden, w_down[col_range, :], preferred_element_type=jnp.float32)
        feed_sum = feed_sum + lax.optimization_barrier(partial_out.astype(jnp.bfloat16)).astype(jnp.float32)
    return layer_norm(second_res + 0.5 * feed_sum, gain_final).astype(jnp.bfloat16)
```

```python
import jax
import jax.numpy as jnp
from jax import lax
from jax.experimental import pallas as pl
from jax.experimental.pallas import tpu as pltpu
from jax.sharding import PartitionSpec as P

HD = 64
C = 128
LANES = 128
EPSILON = 1e-05
NEGATIVE = -1e30
EDGE = 16
MIB = 1 << 20
VMEM = pl.BlockSpec(memory_space=pltpu.VMEM)
ANY = pl.BlockSpec(memory_space=pl.ANY)


def params(limit):
    return pltpu.CompilerParams(vmem_limit_bytes=limit * MIB)


def cost(macs, read):
    return pl.CostEstimate(flops=2 * macs, bytes_accessed=read, transcendentals=0)


def norm_rows(values, gain):
    centred = values - jnp.mean(values, axis=-1, keepdims=True)
    variance = jnp.mean(centred * centred, axis=-1, keepdims=True)
    return centred * lax.rsqrt(variance + EPSILON) * gain


def sigmoid(values):
    return 0.5 + 0.5 * jnp.tanh(0.5 * values)


def each(rows, step, body):
    for first in range(0, rows, step):
        body(slice(first, first + step))


def send_kernel(frames_ref, gain_ref, out_ref, held, sem):
    rows = out_ref.shape[0]
    first = pl.multiple_of(lax.axis_index("mp") * rows, rows)
    copy = pltpu.make_async_copy(frames_ref.at[pl.ds(first, rows)], held, sem)
    copy.start()
    copy.wait()

    def body(part):
        out_ref[part] = norm_rows(held[part].astype(jnp.float32), gain_ref[...]).astype(
            jnp.bfloat16
        )

    each(rows, 16, body)


def own_kernel(frames_ref, gain_ref, w_ref, lengths_ref, context_ref, qkv_ref, flags_ref, normed):
    rows = frames_ref.shape[0]
    step = pl.program_id(0)

    @pl.when(step == 0)
    def _():
        def body(part):
            normed[part] = norm_rows(
                frames_ref[part].astype(jnp.float32), gain_ref[...]
            ).astype(jnp.bfloat16)

        each(rows, 16, body)
        count = lengths_ref.shape[1]
        lengths = jnp.broadcast_to(lengths_ref[...], (8, count))
        before = (
            lax.broadcasted_iota(jnp.int32, (count, count), 0)
            < lax.broadcasted_iota(jnp.int32, (count, count), 1)
        ).astype(jnp.float32).astype(jnp.bfloat16)
        start = jnp.dot(
            lengths.astype(jnp.float32).astype(jnp.bfloat16),
            before,
            preferred_element_type=jnp.float32,
        )
        stretch = (
            lax.axis_index("tm") * (rows // C)
            - 2
            + lax.broadcasted_iota(jnp.int32, (8, count), 0)
        ).astype(jnp.float32)
        end = start + lengths.astype(jnp.float32)
        member = jnp.where((start <= stretch) & (stretch < end), 1.0, 0.0)
        context = jnp.broadcast_to(context_ref[...], (8, count)).astype(jnp.float32)
        number = lax.broadcasted_iota(jnp.int32, (8, count), 1).astype(jnp.float32) + 1.0
        opening = jnp.sum(member * start, axis=1, keepdims=True)
        reached = jnp.sum(member * context, axis=1, keepdims=True)
        label = jnp.sum(member * number, axis=1, keepdims=True)
        flags_ref[0] = jnp.maximum(stretch[:, :LANES] - reached, opening)
        flags_ref[1] = jnp.broadcast_to(label, (8, LANES))

    scale = jnp.where(step == 0, HD**-0.5, 1.0)
    qkv_ref[0] = (
        jnp.dot(normed[...], w_ref[0], preferred_element_type=jnp.float32) * scale
    ).astype(jnp.bfloat16)


def bias_row(lowest, stretches):
    return jnp.concatenate(
        [jnp.where(stretch >= lowest, 0.0, NEGATIVE) for stretch in stretches], axis=1
    )


def attend(query, keys, values, bias):
    first_head = lax.broadcasted_iota(jnp.int32, (C, LANES), 1) < HD
    zero = jnp.zeros_like(query)
    both = jnp.concatenate(
        [jnp.where(first_head, query, zero), jnp.where(first_head, zero, query)], axis=0
    )
    scores = lax.dot_general(
        both, keys, (((1,), (1,)), ((), ())), preferred_element_type=jnp.float32
    )
    scores = scores + bias
    highest = jnp.max(scores, axis=1, keepdims=True)
    raised = jnp.exp(scores - highest).astype(jnp.bfloat16)
    wide = jnp.concatenate([values, jnp.ones_like(values)], axis=1)
    mixed = jnp.dot(raised, wide, preferred_element_type=jnp.float32)
    total = jnp.where(first_head, mixed[:C, :LANES], mixed[C:, :LANES])
    weight = jnp.where(first_head, mixed[:C, LANES:], mixed[C:, LANES:])
    top = jnp.where(
        first_head,
        jnp.broadcast_to(highest[:C], (C, LANES)),
        jnp.broadcast_to(highest[C:], (C, LANES)),
    )
    return total, top, weight


def place(normed, mine_ref, theirs_ref):
    rows = mine_ref.shape[0]
    core = lax.axis_index("mp")
    normed[pl.ds(pl.multiple_of(core * rows, rows), rows)] = mine_ref[...]
    normed[pl.ds(pl.multiple_of((1 - core) * rows, rows), rows)] = theirs_ref[...]


def near_kernel(
    qkv_ref, mine_ref, theirs_ref, w_ref, flags_ref, total_ref, top_ref, weight_ref,
    normed, keys, values,
):
    slab = qkv_ref.shape[1]
    width = qkv_ref.shape[2]
    count = slab // C
    place(normed, mine_ref, theirs_ref)
    keys[slab:] = qkv_ref[1]
    values[slab:] = qkv_ref[2]
    keys[:slab] = jnp.dot(normed[...], w_ref[1], preferred_element_type=jnp.float32).astype(
        jnp.bfloat16
    )
    values[:slab] = jnp.dot(normed[...], w_ref[2], preferred_element_type=jnp.float32).astype(
        jnp.bfloat16
    )
    first = lax.axis_index("tm") * count - count
    for i in range(count):
        rows = slice(i * C, (i + 1) * C)
        seen = count + i + 1
        lowest = flags_ref[0, 2 + i : 3 + i, :]
        bias = bias_row(lowest, [(first + n).astype(jnp.float32) for n in range(seen)])
        for pair in range(width // LANES):
            cols = slice(pair * LANES, (pair + 1) * LANES)
            total_ref[rows, cols], top_ref[rows, cols], weight_ref[rows, cols] = attend(
                qkv_ref[0, rows, cols], keys[: seen * C, cols], values[: seen * C, cols], bias
            )


def far_kernel(
    q_ref, mine_ref, theirs_ref, w_ref, flags_ref, total_ref, top_ref, weight_ref, w_out_ref,
    heads_ref, sent_ref, normed, keys, values,
):
    slab = q_ref.shape[0]
    width = q_ref.shape[1]
    count = slab // C
    place(normed, mine_ref, theirs_ref)
    keys[...] = jnp.dot(normed[...], w_ref[1], preferred_element_type=jnp.float32).astype(
        jnp.bfloat16
    )
    values[...] = jnp.dot(normed[...], w_ref[2], preferred_element_type=jnp.float32).astype(
        jnp.bfloat16
    )
    first = lax.axis_index("tm") * count - 2 * count
    for i in range(count):
        rows = slice(i * C, (i + 1) * C)
        lowest = flags_ref[0, 2 + i : 3 + i, :]
        bias = bias_row(lowest, [(first + n).astype(jnp.float32) for n in range(i, count)])
        for pair in range(width // LANES):
            cols = slice(pair * LANES, (pair + 1) * LANES)
            total, top, weight = attend(
                q_ref[rows, cols], keys[i * C :, cols], values[i * C :, cols], bias
            )
            near_top = top_ref[rows, cols]
            highest = jnp.maximum(near_top, top)
            near_part = jnp.exp(near_top - highest)
            far_part = jnp.exp(top - highest)
            heads_ref[rows, cols] = (
                (total_ref[rows, cols] * near_part + total * far_part)
                / (weight_ref[rows, cols] * near_part + weight * far_part)
            ).astype(jnp.bfloat16)
    window = sent_ref.shape[0]
    other = (1 - lax.axis_index("mp")) * (slab - window)
    sent_ref[...] = jnp.dot(
        heads_ref[pl.ds(pl.multiple_of(other, EDGE), window)],
        w_out_ref[...],
        preferred_element_type=jnp.float32,
    ).astype(jnp.bfloat16)


def base_kernel(heads_ref, w_out_ref, frames_ref, base_ref):
    slab = heads_ref.shape[0]
    window = base_ref.shape[0]
    first = pl.multiple_of(lax.axis_index("mp") * (slab - window), EDGE)
    base_ref[...] = frames_ref[pl.ds(first, window)].astype(jnp.float32) + jnp.dot(
        heads_ref[pl.ds(first, window)], w_out_ref[...], preferred_element_type=jnp.float32
    ).astype(jnp.bfloat16).astype(jnp.float32)


def gate_kernel(
    base_ref, got_ref, gain_ref, w_ref, gated_ref, edge_ref, first_ref, normed, held
):
    window, width = base_ref.shape
    rows = first_ref.shape[0]

    def body(part):
        value = base_ref[part] + got_ref[part].astype(jnp.float32)
        held[part] = value
        normed[part] = norm_rows(value, gain_ref[...]).astype(jnp.bfloat16)

    each(window, 16, body)
    for part in range(0, width, 256):
        cols = slice(part, part + 256)
        value = jnp.dot(normed[...], w_ref[:, cols], preferred_element_type=jnp.float32)
        gate = jnp.dot(
            normed[...],
            w_ref[:, width + part : width + part + 256],
            preferred_element_type=jnp.float32,
        )
        gated_ref[:, cols] = (value * sigmoid(gate)).astype(jnp.bfloat16)
    core = lax.axis_index("mp")
    edge_ref[...] = gated_ref[pl.ds(pl.multiple_of(core * (window - EDGE), EDGE), EDGE)]
    first_ref[...] = held[pl.ds(pl.multiple_of(core * (window - rows), EDGE), rows)]


def conv_kernel(gated_ref, taps_ref, flags_ref, sum_ref, held, padded):
    window, width = gated_ref.shape
    rows = sum_ref.shape[0]
    half = (taps_ref.shape[0] - 1) // 2
    core = lax.axis_index("mp")
    zeros = jnp.zeros((EDGE, width), jnp.float32)
    held[:EDGE] = zeros
    held[rows + EDGE :] = zeros
    held[pl.ds(pl.multiple_of((1 - core) * EDGE, EDGE), window)] = gated_ref[...].astype(
        jnp.float32
    )
    taps = taps_ref[...].astype(jnp.float32)
    for stretch in range(rows // C):
        at = 2 + (rows // C) * core + stretch
        label = flags_ref[1, pl.ds(at, 1), :]
        before = jnp.where(flags_ref[1, pl.ds(at - 1, 1), :] == label, 1.0, 0.0)
        after = jnp.where(flags_ref[1, pl.ds(at + 1, 1), :] == label, 1.0, 0.0)
        low = stretch * C
        for chunk in range(width // LANES):
            cols = slice(chunk * LANES, (chunk + 1) * LANES)
            padded[chunk, :EDGE] = held[low : low + EDGE, cols] * before
            padded[chunk, EDGE : EDGE + C] = held[low + EDGE : low + EDGE + C, cols]
            padded[chunk, EDGE + C :] = held[low + EDGE + C : low + 2 * EDGE + C, cols] * after
        for chunk in range(width // LANES):
            cols = slice(chunk * LANES, (chunk + 1) * LANES)
            for part in range(0, C, 64):
                total = jnp.zeros((64, LANES), jnp.float32)
                for tap in range(taps_ref.shape[0]):
                    at_row = EDGE - half + part + tap
                    total = total + padded[chunk, at_row : at_row + 64] * taps[tap : tap + 1, cols]
                sum_ref[low + part : low + part + 64, cols] = total


def tail_kernel(
    sum_ref, halo_ref, taps_ref, flags_ref, first_ref, gain_depth_ref, gain_ffn_ref, gain_final_ref,
    w_point_ref, up_own_ref, up_other_ref, down_own_ref, down_other_ref,
    out_ref,
    w_point, up, down, around, depth, normed, second, hidden, feed, point_sem, up_sem, down_sem,
):
    rows, width = sum_ref.shape
    half = (taps_ref.shape[0] - 1) // 2
    units = up_own_ref.shape[1]
    step = 512
    point_copy = pltpu.make_async_copy(w_point_ref, w_point, point_sem)
    point_copy.start()
    up_copies, down_copies = [], []
    for group, ref in enumerate((up_own_ref, up_other_ref)):
        for part in range(units // step):
            copy = pltpu.make_async_copy(
                ref.at[:, part * step : (part + 1) * step],
                up.at[group, :, part * step : (part + 1) * step],
                up_sem.at[group, part],
            )
            copy.start()
            up_copies.append(copy)
    for part in range(width // 256):
        for group, ref in enumerate((down_own_ref, down_other_ref)):
            copy = pltpu.make_async_copy(
                ref.at[:, part * 256 : (part + 1) * 256],
                down.at[group, :, part * 256 : (part + 1) * 256],
                down_sem.at[group, part],
            )
            copy.start()
            down_copies.append(copy)

    core = lax.axis_index("mp")
    at = 2 + 3 * core
    same = jnp.where(
        flags_ref[1, pl.ds(at, 1), :] == flags_ref[1, pl.ds(at - 1 + 2 * core, 1), :], 1.0, 0.0
    )
    taps = taps_ref[...].astype(jnp.float32)
    depth[...] = sum_ref[...]
    around[...] = jnp.zeros_like(around)
    for chunk in range(width // LANES):
        cols = slice(chunk * LANES, (chunk + 1) * LANES)
        around[chunk, pl.ds(pl.multiple_of(core * 2 * EDGE, EDGE), EDGE)] = (
            halo_ref[:, cols].astype(jnp.float32) * same
        )
    edge = pl.ds(pl.multiple_of(core * (rows - EDGE), EDGE), EDGE)
    for chunk in range(width // LANES):
        cols = slice(chunk * LANES, (chunk + 1) * LANES)
        total = jnp.zeros((EDGE, LANES), jnp.float32)
        for tap in range(taps_ref.shape[0]):
            at_row = EDGE - half + tap
            total = total + around[chunk, at_row : at_row + EDGE] * taps[tap : tap + 1, cols]
        depth[edge, cols] = depth[edge, cols] + total

    def squash(part):
        value = norm_rows(depth[part], gain_depth_ref[...])
        normed[part] = (value * sigmoid(value)).astype(jnp.bfloat16)

    each(rows, 16, squash)
    point_copy.wait()
    second[...] = first_ref[...] + jnp.dot(
        normed[...], w_point[...], preferred_element_type=jnp.float32
    )

    def ffn_norm(part):
        normed[part] = norm_rows(second[part], gain_ffn_ref[...]).astype(jnp.bfloat16)

    each(rows, 16, ffn_norm)
    for copy, (group, part) in zip(
        up_copies, [(g, p) for g in range(2) for p in range(units // step)]
    ):
        copy.wait()
        cols = slice(part * step, (part + 1) * step)
        value = jnp.dot(normed[...], up[group, :, cols], preferred_element_type=jnp.float32)
        hidden[group, :, cols] = (value * sigmoid(value)).astype(jnp.bfloat16)
    for part in range(width // 256):
        cols = slice(part * 256, (part + 1) * 256)
        total = 0.0
        for group in range(2):
            down_copies[2 * part + group].wait()
            total = total + jnp.dot(
                hidden[group], down[group, :, cols], preferred_element_type=jnp.float32
            ).astype(jnp.bfloat16).astype(jnp.float32)
        feed[:, cols] = second[:, cols] + 0.5 * total

    def finish(part):
        out_ref[part] = norm_rows(feed[part], gain_final_ref[...]).astype(jnp.bfloat16)

    each(rows, 16, finish)


def on_device(
    frames,
    gain_attn,
    w_qkv,
    w_out,
    gain_conv,
    w_point_in,
    w_depth,
    gain_depth,
    w_point_out,
    gain_ffn,
    w_up,
    w_down,
    gain_final,
    lengths,
    context,
):
    slab, width = frames.shape
    rows = slab // 2
    local = w_qkv.shape[2]
    window = rows + EDGE
    units = w_up.shape[1]
    tm = lax.axis_size("tm")
    bf16, f32 = jnp.bfloat16, jnp.float32
    shape = jax.ShapeDtypeStruct
    swap = [(0, 1), (1, 0)]

    def row(vec):
        return vec.reshape(1, -1)

    w_planes = jnp.transpose(w_qkv, (1, 0, 2))
    sent = pl.pallas_call(
        send_kernel,
        out_shape=shape((rows, width), bf16),
        in_specs=[ANY, VMEM],
        out_specs=VMEM,
        scratch_shapes=[pltpu.VMEM((rows, width), bf16), pltpu.SemaphoreType.DMA],
        compiler_params=params(8),
        cost_estimate=cost(0, 2 * rows * width * 2),
        name="send_norm",
    )(frames, row(gain_attn))
    near_mine = lax.ppermute(sent, "tm", [(i, i + 1) for i in range(tm - 1)])
    far_mine = lax.ppermute(sent, "tm", [(i, i + 2) for i in range(tm - 2)])
    up_other = lax.ppermute(w_up, "mp", swap)
    down_other = lax.ppermute(w_down, "mp", swap)
    qkv, flags = pl.pallas_call(
        own_kernel,
        grid=(3,),
        out_shape=(shape((3, slab, local), bf16), shape((2, 8, LANES), f32)),
        in_specs=[
            pl.BlockSpec((slab, width), lambda i: (0, 0)),
            pl.BlockSpec((1, width), lambda i: (0, 0)),
            pl.BlockSpec((1, width, local), lambda i: (i, 0, 0)),
            pl.BlockSpec((1, lengths.shape[0]), lambda i: (0, 0)),
            pl.BlockSpec((1, lengths.shape[0]), lambda i: (0, 0)),
        ],
        out_specs=(
            pl.BlockSpec((1, slab, local), lambda i: (i, 0, 0)),
            pl.BlockSpec((2, 8, LANES), lambda i: (0, 0, 0)),
        ),
        scratch_shapes=[pltpu.VMEM((slab, width), bf16)],
        compiler_params=params(16),
        cost_estimate=cost(slab * width * 3 * local, width * 3 * local * 2),
        name="own_qkv",
    )(frames, row(gain_attn), w_planes, row(lengths), row(context))
    near_theirs = lax.ppermute(near_mine, "mp", swap)
    total, top, weight = pl.pallas_call(
        near_kernel,
        out_shape=(shape((slab, local), f32),) * 3,
        in_specs=[VMEM] * 5,
        out_specs=(VMEM,) * 3,
        scratch_shapes=[
            pltpu.VMEM((slab, width), bf16),
            pltpu.VMEM((2 * slab, local), bf16),
            pltpu.VMEM((2 * slab, local), bf16),
        ],
        compiler_params=params(24),
        cost_estimate=cost(slab * width * 2 * local + 6 * slab * slab * local, 8 * MIB),
        name="near_attention",
    )(qkv, near_mine, near_theirs, w_planes, flags)
    far_theirs = lax.ppermute(far_mine, "mp", swap)
    heads, to_other = pl.pallas_call(
        far_kernel,
        out_shape=(shape((slab, local), bf16), shape((window, width), bf16)),
        in_specs=[VMEM] * 9,
        out_specs=(VMEM,) * 2,
        scratch_shapes=[
            pltpu.VMEM((slab, width), bf16),
            pltpu.VMEM((slab, local), bf16),
            pltpu.VMEM((slab, local), bf16),
        ],
        compiler_params=params(24),
        cost_estimate=cost(slab * width * 2 * local + 3 * slab * slab * local, 10 * MIB),
        name="far_attention",
    )(qkv[0], far_mine, far_theirs, w_planes, flags, total, top, weight, w_out)
    from_other = lax.ppermute(to_other, "mp", swap)
    base = pl.pallas_call(
        base_kernel,
        out_shape=shape((window, width), f32),
        in_specs=[VMEM] * 3,
        out_specs=VMEM,
        compiler_params=params(12),
        cost_estimate=cost(window * width * local, 3 * MIB),
        name="out_projection",
    )(heads, w_out, frames)
    gated, edge, first_res = pl.pallas_call(
        gate_kernel,
        out_shape=(
            shape((window, width), bf16),
            shape((EDGE, width), bf16),
            shape((rows, width), f32),
        ),
        in_specs=[VMEM] * 4,
        out_specs=(VMEM,) * 3,
        scratch_shapes=[pltpu.VMEM((window, width), bf16), pltpu.VMEM((window, width), f32)],
        compiler_params=params(16),
        cost_estimate=cost(window * width * 2 * width, 5 * MIB),
        name="gated_units",
    )(base, from_other, row(gain_conv), w_point_in)
    halo_pairs = [(2 * i + 1, 2 * i + 2) for i in range(tm - 1)]
    halo = lax.ppermute(edge, ("tm", "mp"), halo_pairs + [(b, a) for a, b in halo_pairs])
    depth_sum = pl.pallas_call(
        conv_kernel,
        out_shape=shape((rows, width), f32),
        in_specs=[VMEM] * 3,
        out_specs=VMEM,
        scratch_shapes=[
            pltpu.VMEM((rows + 2 * EDGE, width), f32),
            pltpu.VMEM((width // LANES, C + 2 * EDGE, LANES), f32),
        ],
        compiler_params=params(12),
        cost_estimate=cost(rows * width * 512, MIB),
        name="depthwise",
    )(gated, w_depth, flags)
    return pl.pallas_call(
        tail_kernel,
        out_shape=shape((rows, width), bf16),
        in_specs=[VMEM] * 8 + [ANY] * 5,
        out_specs=VMEM,
        scratch_shapes=[
            pltpu.VMEM((width, width), bf16),
            pltpu.VMEM((2, width, units), bf16),
            pltpu.VMEM((2, units, width), bf16),
            pltpu.VMEM((width // LANES, 3 * EDGE, LANES), f32),
            pltpu.VMEM((rows, width), f32),
            pltpu.VMEM((rows, width), bf16),
            pltpu.VMEM((rows, width), f32),
            pltpu.VMEM((2, rows, units), bf16),
            pltpu.VMEM((rows, width), f32),
            pltpu.SemaphoreType.DMA,
            pltpu.SemaphoreType.DMA((2, units // 512)),
            pltpu.SemaphoreType.DMA((2, width // 256)),
        ],
        compiler_params=params(40),
        cost_estimate=cost(rows * width * 9 * width, 18 * MIB),
        name="tail",
    )(
        depth_sum, halo, w_depth, flags, first_res, row(gain_depth), row(gain_ffn),
        row(gain_final), w_point_out, w_up, up_other, w_down, down_other,
    )


def solution(mesh):
    in_specs = (
        P("tm", None),
        P(),
        P(None, None, "mp"),
        P("mp", None),
        P(),
        P(),
        P(),
        P(),
        P(),
        P(),
        P(None, "mp"),
        P("mp", None),
        P(),
        P(),
        P(),
    )
    out_specs = P(("tm", "mp"), None)
    return jax.shard_map(
        on_device, mesh=mesh, in_specs=in_specs, out_specs=out_specs, check_vma=False
    )
```

```python
import jax
import jax.numpy as jnp
from jax import lax
from jax.experimental import pallas as pl
from jax.experimental.pallas import tpu as pltpu
from jax.sharding import PartitionSpec as P

HD = 64
C = 128
LANES = 128
EPSILON = 1e-05
NEGATIVE = -1e30
EDGE = 16
MIB = 1 << 20
EARLY = 0.001
LATE = 4.0
VMEM = pl.BlockSpec(memory_space=pltpu.VMEM)
HBM = pl.BlockSpec(memory_space=pltpu.HBM)


def params(limit):
    return pltpu.CompilerParams(vmem_limit_bytes=limit * MIB)


def cost(macs, read, share=1.0):
    return pl.CostEstimate(
        flops=int(2 * macs * share), bytes_accessed=int(read * share), transcendentals=0
    )


def norm_rows(values, gain):
    centred = values - jnp.mean(values, axis=-1, keepdims=True)
    variance = jnp.mean(centred * centred, axis=-1, keepdims=True)
    return centred * lax.rsqrt(variance + EPSILON) * gain


def sigmoid(values):
    return 0.5 + 0.5 * jnp.tanh(0.5 * values)


def each(rows, step, body):
    for first in range(0, rows, step):
        body(slice(first, first + step))


def send_kernel(frames_ref, gain_ref, out_ref, held, gain, sem):
    rows = out_ref.shape[0]
    first = pl.multiple_of(lax.axis_index("mp") * rows, rows)
    copies = [
        pltpu.make_async_copy(gain_ref, gain, sem.at[0]),
        pltpu.make_async_copy(frames_ref.at[pl.ds(first, rows)], held, sem.at[1]),
    ]
    for copy in copies:
        copy.start()
    for copy in copies:
        copy.wait()

    def body(part):
        out_ref[part] = norm_rows(held[part].astype(jnp.float32), gain[...]).astype(jnp.bfloat16)

    each(rows, 16, body)


def own_kernel(frames_ref, gain_ref, w_ref, lengths_ref, context_ref, qkv_ref, flags_ref, normed):
    rows = frames_ref.shape[0]
    step = pl.program_id(0)

    @pl.when(step == 0)
    def _():
        def body(part):
            normed[part] = norm_rows(
                frames_ref[part].astype(jnp.float32), gain_ref[...]
            ).astype(jnp.bfloat16)

        each(rows, 16, body)
        count = lengths_ref.shape[1]
        lengths = jnp.broadcast_to(lengths_ref[...], (8, count))
        before = (
            lax.broadcasted_iota(jnp.int32, (count, count), 0)
            < lax.broadcasted_iota(jnp.int32, (count, count), 1)
        ).astype(jnp.float32).astype(jnp.bfloat16)
        start = jnp.dot(
            lengths.astype(jnp.float32).astype(jnp.bfloat16),
            before,
            preferred_element_type=jnp.float32,
        )
        stretch = (
            lax.axis_index("tm") * (rows // C)
            - 2
            + lax.broadcasted_iota(jnp.int32, (8, count), 0)
        ).astype(jnp.float32)
        end = start + lengths.astype(jnp.float32)
        member = jnp.where((start <= stretch) & (stretch < end), 1.0, 0.0)
        context = jnp.broadcast_to(context_ref[...], (8, count)).astype(jnp.float32)
        number = lax.broadcasted_iota(jnp.int32, (8, count), 1).astype(jnp.float32) + 1.0
        opening = jnp.sum(member * start, axis=1, keepdims=True)
        reached = jnp.sum(member * context, axis=1, keepdims=True)
        label = jnp.sum(member * number, axis=1, keepdims=True)
        flags_ref[0] = jnp.maximum(stretch[:, :LANES] - reached, opening)
        flags_ref[1] = jnp.broadcast_to(label, (8, LANES))

    scale = jnp.where(step == 0, HD**-0.5, 1.0)
    qkv_ref[0] = (
        jnp.dot(normed[...], w_ref[0], preferred_element_type=jnp.float32) * scale
    ).astype(jnp.bfloat16)


def bias_row(lowest, stretches):
    return jnp.concatenate(
        [jnp.where(stretch >= lowest, 0.0, NEGATIVE) for stretch in stretches], axis=1
    )


def attend(query, keys, values, bias):
    first_head = lax.broadcasted_iota(jnp.int32, (C, LANES), 1) < HD
    zero = jnp.zeros_like(query)
    both = jnp.concatenate(
        [jnp.where(first_head, query, zero), jnp.where(first_head, zero, query)], axis=0
    )
    scores = lax.dot_general(
        both, keys, (((1,), (1,)), ((), ())), preferred_element_type=jnp.float32
    )
    scores = scores + bias
    highest = jnp.max(scores, axis=1, keepdims=True)
    raised = jnp.exp(scores - highest).astype(jnp.bfloat16)
    wide = jnp.concatenate([values, jnp.ones_like(values)], axis=1)
    mixed = jnp.dot(raised, wide, preferred_element_type=jnp.float32)
    total = jnp.where(first_head, mixed[:C, :LANES], mixed[C:, :LANES])
    weight = jnp.where(first_head, mixed[:C, LANES:], mixed[C:, LANES:])
    top = jnp.where(
        first_head,
        jnp.broadcast_to(highest[:C], (C, LANES)),
        jnp.broadcast_to(highest[C:], (C, LANES)),
    )
    return total, top, weight


def place(normed, mine_ref, theirs_ref):
    rows = mine_ref.shape[0]
    core = lax.axis_index("mp")
    normed[pl.ds(pl.multiple_of(core * rows, rows), rows)] = mine_ref[...]
    normed[pl.ds(pl.multiple_of((1 - core) * rows, rows), rows)] = theirs_ref[...]


def merged(parts, total, top, weight):
    other_total, other_top, other_weight = parts
    highest = jnp.maximum(other_top, top)
    other_part = jnp.exp(other_top - highest)
    part = jnp.exp(top - highest)
    return (
        other_total * other_part + total * part,
        highest,
        other_weight * other_part + weight * part,
    )


def self_kernel(qkv_ref, flags_ref, total_ref, top_ref, weight_ref):
    slab, width = qkv_ref.shape[1:]
    count = slab // C
    first = lax.axis_index("tm") * count
    for i in range(count):
        rows = slice(i * C, (i + 1) * C)
        lowest = flags_ref[0, 2 + i : 3 + i, :]
        bias = bias_row(lowest, [(first + n).astype(jnp.float32) for n in range(i + 1)])
        for pair in range(width // LANES):
            cols = slice(pair * LANES, (pair + 1) * LANES)
            seen = slice(0, (i + 1) * C)
            total_ref[rows, cols], top_ref[rows, cols], weight_ref[rows, cols] = attend(
                qkv_ref[0, rows, cols], qkv_ref[1, seen, cols], qkv_ref[2, seen, cols], bias
            )


def near_kernel(
    qkv_ref, mine_ref, theirs_ref, w_ref, flags_ref, own_total_ref, own_top_ref, own_weight_ref,
    total_ref, top_ref, weight_ref,
    normed, keys, values,
):
    slab, width = qkv_ref.shape[1:]
    count = slab // C
    place(normed, mine_ref, theirs_ref)
    keys[...] = jnp.dot(normed[...], w_ref[1], preferred_element_type=jnp.float32).astype(
        jnp.bfloat16
    )
    values[...] = jnp.dot(normed[...], w_ref[2], preferred_element_type=jnp.float32).astype(
        jnp.bfloat16
    )
    first = lax.axis_index("tm") * count - count
    for i in range(count):
        rows = slice(i * C, (i + 1) * C)
        lowest = flags_ref[0, 2 + i : 3 + i, :]
        bias = bias_row(lowest, [(first + n).astype(jnp.float32) for n in range(count)])
        for pair in range(width // LANES):
            cols = slice(pair * LANES, (pair + 1) * LANES)
            parts = own_total_ref[rows, cols], own_top_ref[rows, cols], own_weight_ref[rows, cols]
            total_ref[rows, cols], top_ref[rows, cols], weight_ref[rows, cols] = merged(
                parts, *attend(qkv_ref[0, rows, cols], keys[:, cols], values[:, cols], bias)
            )


def far_kernel(
    qkv_ref, mine_ref, theirs_ref, w_ref, flags_ref, total_ref, top_ref, weight_ref, w_out_ref,
    heads_ref, sent_ref, normed, keys, values,
):
    slab, width = qkv_ref.shape[1:]
    count = slab // C
    place(normed, mine_ref, theirs_ref)
    keys[...] = jnp.dot(normed[...], w_ref[1], preferred_element_type=jnp.float32).astype(
        jnp.bfloat16
    )
    values[...] = jnp.dot(normed[...], w_ref[2], preferred_element_type=jnp.float32).astype(
        jnp.bfloat16
    )
    first = lax.axis_index("tm") * count - 2 * count
    for i in range(count):
        rows = slice(i * C, (i + 1) * C)
        lowest = flags_ref[0, 2 + i : 3 + i, :]
        bias = bias_row(lowest, [(first + n).astype(jnp.float32) for n in range(i, count)])
        for pair in range(width // LANES):
            cols = slice(pair * LANES, (pair + 1) * LANES)
            total, top, weight = attend(
                qkv_ref[0, rows, cols], keys[i * C :, cols], values[i * C :, cols], bias
            )
            parts = total_ref[rows, cols], top_ref[rows, cols], weight_ref[rows, cols]
            total, _, weight = merged(parts, total, top, weight)
            heads_ref[rows, cols] = (total / weight).astype(jnp.bfloat16)
    window = sent_ref.shape[0]
    other = (1 - lax.axis_index("mp")) * (slab - window)
    sent_ref[...] = jnp.dot(
        heads_ref[pl.ds(pl.multiple_of(other, EDGE), window)],
        w_out_ref[...],
        preferred_element_type=jnp.float32,
    ).astype(jnp.bfloat16)


def base_kernel(heads_ref, w_out_ref, frames_ref, base_ref):
    slab = heads_ref.shape[0]
    window = base_ref.shape[0]
    first = pl.multiple_of(lax.axis_index("mp") * (slab - window), EDGE)
    base_ref[...] = frames_ref[pl.ds(first, window)].astype(jnp.float32) + jnp.dot(
        heads_ref[pl.ds(first, window)], w_out_ref[...], preferred_element_type=jnp.float32
    ).astype(jnp.bfloat16).astype(jnp.float32)


def gate_kernel(
    base_ref, got_ref, gain_ref, w_ref, gated_ref, edge_ref, first_ref, normed, held
):
    window, width = base_ref.shape
    rows = first_ref.shape[0]

    def body(part):
        value = base_ref[part] + got_ref[part].astype(jnp.float32)
        held[part] = value
        normed[part] = norm_rows(value, gain_ref[...]).astype(jnp.bfloat16)

    each(window, 16, body)
    for part in range(0, width, 256):
        cols = slice(part, part + 256)
        value = jnp.dot(normed[...], w_ref[:, cols], preferred_element_type=jnp.float32)
        gate = jnp.dot(
            normed[...],
            w_ref[:, width + part : width + part + 256],
            preferred_element_type=jnp.float32,
        )
        gated_ref[:, cols] = (value * sigmoid(gate)).astype(jnp.bfloat16)
    core = lax.axis_index("mp")
    edge_ref[...] = gated_ref[pl.ds(pl.multiple_of(core * (window - EDGE), EDGE), EDGE)]
    first_ref[...] = held[pl.ds(pl.multiple_of(core * (window - rows), EDGE), rows)]


def conv_kernel(gated_ref, taps_ref, flags_ref, sum_ref, held, padded):
    window, width = gated_ref.shape
    rows = sum_ref.shape[0]
    half = (taps_ref.shape[0] - 1) // 2
    core = lax.axis_index("mp")
    zeros = jnp.zeros((EDGE, width), jnp.float32)
    held[:EDGE] = zeros
    held[rows + EDGE :] = zeros
    held[pl.ds(pl.multiple_of((1 - core) * EDGE, EDGE), window)] = gated_ref[...].astype(
        jnp.float32
    )
    taps = taps_ref[...].astype(jnp.float32)
    for stretch in range(rows // C):
        at = 2 + (rows // C) * core + stretch
        label = flags_ref[1, pl.ds(at, 1), :]
        before = jnp.where(flags_ref[1, pl.ds(at - 1, 1), :] == label, 1.0, 0.0)
        after = jnp.where(flags_ref[1, pl.ds(at + 1, 1), :] == label, 1.0, 0.0)
        low = stretch * C
        for chunk in range(width // LANES):
            cols = slice(chunk * LANES, (chunk + 1) * LANES)
            padded[chunk, :EDGE] = held[low : low + EDGE, cols] * before
            padded[chunk, EDGE : EDGE + C] = held[low + EDGE : low + EDGE + C, cols]
            padded[chunk, EDGE + C :] = held[low + EDGE + C : low + 2 * EDGE + C, cols] * after
        for chunk in range(width // LANES):
            cols = slice(chunk * LANES, (chunk + 1) * LANES)
            for part in range(0, C, 64):
                total = jnp.zeros((64, LANES), jnp.float32)
                for tap in range(taps_ref.shape[0]):
                    at_row = EDGE - half + part + tap
                    total = total + padded[chunk, at_row : at_row + 64] * taps[tap : tap + 1, cols]
                sum_ref[low + part : low + part + 64, cols] = total


def tail_kernel(
    sum_ref, halo_ref, taps_ref, flags_ref, first_ref, gain_depth_ref, gain_ffn_ref, gain_final_ref,
    w_point_ref, up_own_ref, up_other_ref, down_own_ref, down_other_ref,
    out_ref,
    down, around, depth, normed, second, hidden, feed, down_sem,
):
    rows, width = sum_ref.shape
    half = (taps_ref.shape[0] - 1) // 2
    units = up_own_ref.shape[1]
    step = 512
    down_copies = []
    for part in range(width // 256):
        for group, ref in enumerate((down_own_ref, down_other_ref)):
            copy = pltpu.make_async_copy(
                ref.at[:, part * 256 : (part + 1) * 256],
                down.at[group, :, part * 256 : (part + 1) * 256],
                down_sem.at[group, part],
            )
            copy.start()
            down_copies.append(copy)

    core = lax.axis_index("mp")
    at = 2 + 3 * core
    same = jnp.where(
        flags_ref[1, pl.ds(at, 1), :] == flags_ref[1, pl.ds(at - 1 + 2 * core, 1), :], 1.0, 0.0
    )
    taps = taps_ref[...].astype(jnp.float32)
    depth[...] = sum_ref[...]
    around[...] = jnp.zeros_like(around)
    for chunk in range(width // LANES):
        cols = slice(chunk * LANES, (chunk + 1) * LANES)
        around[chunk, pl.ds(pl.multiple_of(core * 2 * EDGE, EDGE), EDGE)] = (
            halo_ref[:, cols].astype(jnp.float32) * same
        )
    edge = pl.ds(pl.multiple_of(core * (rows - EDGE), EDGE), EDGE)
    for chunk in range(width // LANES):
        cols = slice(chunk * LANES, (chunk + 1) * LANES)
        total = jnp.zeros((EDGE, LANES), jnp.float32)
        for tap in range(taps_ref.shape[0]):
            at_row = EDGE - half + tap
            total = total + around[chunk, at_row : at_row + EDGE] * taps[tap : tap + 1, cols]
        depth[edge, cols] = depth[edge, cols] + total

    def squash(part):
        value = norm_rows(depth[part], gain_depth_ref[...])
        normed[part] = (value * sigmoid(value)).astype(jnp.bfloat16)

    each(rows, 16, squash)
    second[...] = first_ref[...] + jnp.dot(
        normed[...], w_point_ref[...], preferred_element_type=jnp.float32
    )

    def ffn_norm(part):
        normed[part] = norm_rows(second[part], gain_ffn_ref[...]).astype(jnp.bfloat16)

    each(rows, 16, ffn_norm)
    for group, ref in enumerate((up_own_ref, up_other_ref)):
        for part in range(units // step):
            cols = slice(part * step, (part + 1) * step)
            value = jnp.dot(normed[...], ref[:, cols], preferred_element_type=jnp.float32)
            hidden[group, :, cols] = (value * sigmoid(value)).astype(jnp.bfloat16)
    for part in range(width // 256):
        cols = slice(part * 256, (part + 1) * 256)
        total = 0.0
        for group in range(2):
            down_copies[2 * part + group].wait()
            total = total + jnp.dot(
                hidden[group], down[group, :, cols], preferred_element_type=jnp.float32
            ).astype(jnp.bfloat16).astype(jnp.float32)
        feed[:, cols] = second[:, cols] + 0.5 * total

    def finish(part):
        out_ref[part] = norm_rows(feed[part], gain_final_ref[...]).astype(jnp.bfloat16)

    each(rows, 16, finish)


def on_device(
    frames,
    gain_attn,
    w_qkv,
    w_out,
    gain_conv,
    w_point_in,
    w_depth,
    gain_depth,
    w_point_out,
    gain_ffn,
    w_up,
    w_down,
    gain_final,
    lengths,
    context,
):
    slab, width = frames.shape
    rows = slab // 2
    local = w_qkv.shape[2]
    window = rows + EDGE
    units = w_up.shape[1]
    tm = lax.axis_size("tm")
    bf16, f32 = jnp.bfloat16, jnp.float32
    shape = jax.ShapeDtypeStruct
    swap = [(0, 1), (1, 0)]

    def row(vec):
        return vec.reshape(1, -1)

    w_planes = jnp.transpose(w_qkv, (1, 0, 2))
    sent = pl.pallas_call(
        send_kernel,
        out_shape=shape((rows, width), bf16),
        in_specs=[HBM, HBM],
        out_specs=VMEM,
        scratch_shapes=[
            pltpu.VMEM((rows, width), bf16),
            pltpu.VMEM((1, width), f32),
            pltpu.SemaphoreType.DMA((2,)),
        ],
        compiler_params=params(8),
        cost_estimate=cost(0, 2 * rows * width * 2),
        name="send_norm",
    )(frames, row(gain_attn))
    own_frames, sent = lax.optimization_barrier((frames, sent))
    near_mine = lax.ppermute(sent, "tm", [(i, i + 1) for i in range(tm - 1)])
    qkv, flags = pl.pallas_call(
        own_kernel,
        grid=(3,),
        out_shape=(shape((3, slab, local), bf16), shape((2, 8, LANES), f32)),
        in_specs=[
            pl.BlockSpec((slab, width), lambda i: (0, 0)),
            pl.BlockSpec((1, width), lambda i: (0, 0)),
            pl.BlockSpec((1, width, local), lambda i: (i, 0, 0)),
            pl.BlockSpec((1, lengths.shape[0]), lambda i: (0, 0)),
            pl.BlockSpec((1, lengths.shape[0]), lambda i: (0, 0)),
        ],
        out_specs=(
            pl.BlockSpec((1, slab, local), lambda i: (i, 0, 0)),
            pl.BlockSpec((2, 8, LANES), lambda i: (0, 0, 0)),
        ),
        scratch_shapes=[pltpu.VMEM((slab, width), bf16)],
        compiler_params=params(16),
        cost_estimate=cost(slab * width * 3 * local, width * 3 * local * 2, EARLY),
        name="own_qkv",
    )(own_frames, row(gain_attn), w_planes, row(lengths), row(context))
    partial = (shape((slab, local), f32),) * 3
    own_parts = pl.pallas_call(
        self_kernel,
        out_shape=partial,
        in_specs=[VMEM] * 2,
        out_specs=(VMEM,) * 3,
        compiler_params=params(16),
        cost_estimate=cost(5 * slab * slab * local, 4 * MIB, EARLY),
        name="own_attention",
    )(qkv, flags)
    up_held, down_held, own_parts = lax.optimization_barrier((w_up, w_down, own_parts))
    up_other = lax.ppermute(up_held, "mp", swap)
    down_other = lax.ppermute(down_held, "mp", swap)
    near_mine, own_parts = lax.optimization_barrier((near_mine, own_parts))
    far_mine = lax.ppermute(near_mine, "tm", [(i, i + 1) for i in range(tm - 1)])
    near_theirs = lax.ppermute(near_mine, "mp", swap)
    near_parts = pl.pallas_call(
        near_kernel,
        out_shape=partial,
        in_specs=[VMEM] * 8,
        out_specs=(VMEM,) * 3,
        scratch_shapes=[
            pltpu.VMEM((slab, width), bf16),
            pltpu.VMEM((slab, local), bf16),
            pltpu.VMEM((slab, local), bf16),
        ],
        compiler_params=params(16),
        cost_estimate=cost(slab * width * 2 * local + 8 * slab * slab * local, 8 * MIB, LATE),
        name="near_attention",
    )(qkv, near_mine, near_theirs, w_planes, flags, *own_parts)
    far_mine, near_parts = lax.optimization_barrier((far_mine, near_parts))
    far_theirs = lax.ppermute(far_mine, "mp", swap)
    heads, to_other = pl.pallas_call(
        far_kernel,
        out_shape=(shape((slab, local), bf16), shape((window, width), bf16)),
        in_specs=[VMEM] * 9,
        out_specs=(VMEM,) * 2,
        scratch_shapes=[
            pltpu.VMEM((slab, width), bf16),
            pltpu.VMEM((slab, local), bf16),
            pltpu.VMEM((slab, local), bf16),
        ],
        compiler_params=params(16),
        cost_estimate=cost(slab * width * 2 * local + 3 * slab * slab * local, 10 * MIB, LATE),
        name="far_attention",
    )(qkv, far_mine, far_theirs, w_planes, flags, *near_parts, w_out)
    from_other = lax.ppermute(to_other, "mp", swap)
    base = pl.pallas_call(
        base_kernel,
        out_shape=shape((window, width), f32),
        in_specs=[VMEM] * 3,
        out_specs=VMEM,
        compiler_params=params(12),
        cost_estimate=cost(window * width * local, 3 * MIB, LATE),
        name="out_projection",
    )(heads, w_out, frames)
    gated, edge, first_res = pl.pallas_call(
        gate_kernel,
        out_shape=(
            shape((window, width), bf16),
            shape((EDGE, width), bf16),
            shape((rows, width), f32),
        ),
        in_specs=[VMEM] * 4,
        out_specs=(VMEM,) * 3,
        scratch_shapes=[pltpu.VMEM((window, width), bf16), pltpu.VMEM((window, width), f32)],
        compiler_params=params(16),
        cost_estimate=cost(window * width * 2 * width, 5 * MIB, LATE),
        name="gated_units",
    )(base, from_other, row(gain_conv), w_point_in)
    halo_pairs = [(2 * i + 1, 2 * i + 2) for i in range(tm - 1)]
    halo = lax.ppermute(edge, ("tm", "mp"), halo_pairs + [(b, a) for a, b in halo_pairs])
    depth_sum = pl.pallas_call(
        conv_kernel,
        out_shape=shape((rows, width), f32),
        in_specs=[VMEM] * 3,
        out_specs=VMEM,
        scratch_shapes=[
            pltpu.VMEM((rows + 2 * EDGE, width), f32),
            pltpu.VMEM((width // LANES, C + 2 * EDGE, LANES), f32),
        ],
        compiler_params=params(12),
        cost_estimate=cost(rows * width * 512, MIB, LATE),
        name="depthwise",
    )(gated, w_depth, flags)
    return pl.pallas_call(
        tail_kernel,
        out_shape=shape((rows, width), bf16),
        in_specs=[VMEM] * 11 + [HBM] * 2,
        out_specs=VMEM,
        scratch_shapes=[
            pltpu.VMEM((2, units, width), bf16),
            pltpu.VMEM((width // LANES, 3 * EDGE, LANES), f32),
            pltpu.VMEM((rows, width), f32),
            pltpu.VMEM((rows, width), bf16),
            pltpu.VMEM((rows, width), f32),
            pltpu.VMEM((2, rows, units), bf16),
            pltpu.VMEM((rows, width), f32),
            pltpu.SemaphoreType.DMA((2, width // 256)),
        ],
        compiler_params=params(20),
        cost_estimate=cost(rows * width * 9 * width, 18 * MIB, LATE),
        name="tail",
    )(
        depth_sum, halo, w_depth, flags, first_res, row(gain_depth), row(gain_ffn),
        row(gain_final), w_point_out, w_up, up_other, w_down, down_other,
    )


def solution(mesh):
    in_specs = (
        P("tm", None),
        P(),
        P(None, None, "mp"),
        P("mp", None),
        P(),
        P(),
        P(),
        P(),
        P(),
        P(),
        P(None, "mp"),
        P("mp", None),
        P(),
        P(),
        P(),
    )
    out_specs = P(("tm", "mp"), None)
    return jax.shard_map(
        on_device, mesh=mesh, in_specs=in_specs, out_specs=out_specs, check_vma=False
    )
```

```python
import jax
import jax.numpy as jnp
from jax import lax
from jax.experimental import pallas as pl
from jax.experimental.pallas import tpu as pltpu
from jax.sharding import PartitionSpec as P

HD = 64
C = 128
LANES = 128
EPSILON = 1e-05
NEGATIVE = -1e30
EDGE = 16
MIB = 1 << 20
EARLY = 0.001
LATE = 4.0
MIDDLE = 4.0
VMEM = pl.BlockSpec(memory_space=pltpu.VMEM)
HBM = pl.BlockSpec(memory_space=pltpu.HBM)


def params(limit):
    return pltpu.CompilerParams(vmem_limit_bytes=limit * MIB)


def cost(macs, read, share=1.0):
    return pl.CostEstimate(
        flops=int(2 * macs * share), bytes_accessed=int(read * share), transcendentals=0
    )


def norm_rows(values, gain):
    centred = values - jnp.mean(values, axis=-1, keepdims=True)
    variance = jnp.mean(centred * centred, axis=-1, keepdims=True)
    return centred * lax.rsqrt(variance + EPSILON) * gain


def sigmoid(values):
    return 0.5 + 0.5 * jnp.tanh(0.5 * values)


def each(rows, step, body):
    for first in range(0, rows, step):
        body(slice(first, first + step))


def send_kernel(frames_ref, gain_ref, sent_ref, normed_ref):
    rows = sent_ref.shape[0]

    def body(part):
        normed_ref[part] = norm_rows(
            frames_ref[part].astype(jnp.float32), gain_ref[...]
        ).astype(jnp.bfloat16)

    each(normed_ref.shape[0], 16, body)
    first = pl.multiple_of(lax.axis_index("mp") * rows, rows)
    sent_ref[...] = normed_ref[pl.ds(first, rows)]


def own_kernel(normed_ref, w_ref, lengths_ref, context_ref, qkv_ref, flags_ref):
    rows = normed_ref.shape[0]
    step = pl.program_id(0)

    @pl.when(step == 0)
    def _():
        count = lengths_ref.shape[1]
        lengths = jnp.broadcast_to(lengths_ref[...], (8, count))
        before = (
            lax.broadcasted_iota(jnp.int32, (count, count), 0)
            < lax.broadcasted_iota(jnp.int32, (count, count), 1)
        ).astype(jnp.float32).astype(jnp.bfloat16)
        start = jnp.dot(
            lengths.astype(jnp.float32).astype(jnp.bfloat16),
            before,
            preferred_element_type=jnp.float32,
        )
        stretch = (
            lax.axis_index("tm") * (rows // C)
            - 2
            + lax.broadcasted_iota(jnp.int32, (8, count), 0)
        ).astype(jnp.float32)
        end = start + lengths.astype(jnp.float32)
        member = jnp.where((start <= stretch) & (stretch < end), 1.0, 0.0)
        context = jnp.broadcast_to(context_ref[...], (8, count)).astype(jnp.float32)
        number = lax.broadcasted_iota(jnp.int32, (8, count), 1).astype(jnp.float32) + 1.0
        opening = jnp.sum(member * start, axis=1, keepdims=True)
        reached = jnp.sum(member * context, axis=1, keepdims=True)
        label = jnp.sum(member * number, axis=1, keepdims=True)
        flags_ref[0] = jnp.maximum(stretch[:, :LANES] - reached, opening)
        flags_ref[1] = jnp.broadcast_to(label, (8, LANES))

    scale = jnp.where(step == 0, HD**-0.5, 1.0)
    qkv_ref[0] = (
        jnp.dot(normed_ref[...], w_ref[0], preferred_element_type=jnp.float32) * scale
    ).astype(jnp.bfloat16)


def bias_row(lowest, stretches):
    return jnp.concatenate(
        [jnp.where(stretch >= lowest, 0.0, NEGATIVE) for stretch in stretches], axis=1
    )


def attend_all(queries, keys, values, biases):
    first_head = lax.broadcasted_iota(jnp.int32, (C, LANES), 1) < HD
    zero = jnp.zeros_like(queries[0])
    stacked = []
    for query in queries:
        stacked += [jnp.where(first_head, query, zero), jnp.where(first_head, zero, query)]
    scores = lax.dot_general(
        jnp.concatenate(stacked, axis=0),
        keys,
        (((1,), (1,)), ((), ())),
        preferred_element_type=jnp.float32,
    )
    raised, tops = [], []
    for i, bias in enumerate(biases):
        part = scores[2 * i * C : 2 * (i + 1) * C] + bias
        highest = jnp.max(part, axis=1, keepdims=True)
        raised.append(jnp.exp(part - highest).astype(jnp.bfloat16))
        tops.append(highest)
    wide = jnp.concatenate([values, jnp.ones_like(values)], axis=1)
    mixed = jnp.dot(jnp.concatenate(raised, axis=0), wide, preferred_element_type=jnp.float32)
    found = []
    for i, highest in enumerate(tops):
        one = mixed[2 * i * C : (2 * i + 1) * C]
        two = mixed[(2 * i + 1) * C : 2 * (i + 1) * C]
        total = jnp.where(first_head, one[:, :LANES], two[:, :LANES])
        weight = jnp.where(first_head, one[:, LANES:], two[:, LANES:])
        top = jnp.where(
            first_head,
            jnp.broadcast_to(highest[:C], (C, LANES)),
            jnp.broadcast_to(highest[C:], (C, LANES)),
        )
        found.append((total, top, weight))
    return found


def attend(query, keys, values, bias):
    return attend_all([query], keys, values, [bias])[0]


def place(normed, mine_ref, theirs_ref):
    rows = mine_ref.shape[0]
    core = lax.axis_index("mp")
    normed[pl.ds(pl.multiple_of(core * rows, rows), rows)] = mine_ref[...]
    normed[pl.ds(pl.multiple_of((1 - core) * rows, rows), rows)] = theirs_ref[...]


def merged(parts, total, top, weight):
    other_total, other_top, other_weight = parts
    highest = jnp.maximum(other_top, top)
    other_part = jnp.exp(other_top - highest)
    part = jnp.exp(top - highest)
    return (
        other_total * other_part + total * part,
        highest,
        other_weight * other_part + weight * part,
    )


def self_kernel(qkv_ref, flags_ref, total_ref, top_ref, weight_ref):
    slab, width = qkv_ref.shape[1:]
    count = slab // C
    first = lax.axis_index("tm") * count
    for i in range(count):
        rows = slice(i * C, (i + 1) * C)
        lowest = flags_ref[0, 2 + i : 3 + i, :]
        bias = bias_row(lowest, [(first + n).astype(jnp.float32) for n in range(i + 1)])
        for pair in range(width // LANES):
            cols = slice(pair * LANES, (pair + 1) * LANES)
            seen = slice(0, (i + 1) * C)
            total_ref[rows, cols], top_ref[rows, cols], weight_ref[rows, cols] = attend(
                qkv_ref[0, rows, cols], qkv_ref[1, seen, cols], qkv_ref[2, seen, cols], bias
            )


def near_kernel(
    qkv_ref, mine_ref, theirs_ref, w_ref, flags_ref, own_total_ref, own_top_ref, own_weight_ref,
    total_ref, top_ref, weight_ref,
    normed, keys, values,
):
    slab, width = qkv_ref.shape[1:]
    count = slab // C
    place(normed, mine_ref, theirs_ref)
    keys[...] = jnp.dot(normed[...], w_ref[1], preferred_element_type=jnp.float32).astype(
        jnp.bfloat16
    )
    values[...] = jnp.dot(normed[...], w_ref[2], preferred_element_type=jnp.float32).astype(
        jnp.bfloat16
    )
    first = lax.axis_index("tm") * count - count
    every = [slice(i * C, (i + 1) * C) for i in range(count)]
    seen = [(first + n).astype(jnp.float32) for n in range(count)]
    biases = [bias_row(flags_ref[0, 2 + i : 3 + i, :], seen) for i in range(count)]
    for pair in range(width // LANES):
        cols = slice(pair * LANES, (pair + 1) * LANES)
        found = attend_all(
            [qkv_ref[0, rows, cols] for rows in every], keys[:, cols], values[:, cols], biases
        )
        for rows, part in zip(every, found):
            parts = own_total_ref[rows, cols], own_top_ref[rows, cols], own_weight_ref[rows, cols]
            total_ref[rows, cols], top_ref[rows, cols], weight_ref[rows, cols] = merged(
                parts, *part
            )


def far_kernel(
    qkv_ref, mine_ref, theirs_ref, w_ref, flags_ref, total_ref, top_ref, weight_ref, w_out_ref,
    heads_ref, sent_ref, normed, keys, values,
):
    slab, width = qkv_ref.shape[1:]
    count = slab // C
    place(normed, mine_ref, theirs_ref)
    keys[...] = jnp.dot(normed[...], w_ref[1], preferred_element_type=jnp.float32).astype(
        jnp.bfloat16
    )
    values[...] = jnp.dot(normed[...], w_ref[2], preferred_element_type=jnp.float32).astype(
        jnp.bfloat16
    )
    first = lax.axis_index("tm") * count - 2 * count
    for i in range(count):
        rows = slice(i * C, (i + 1) * C)
        lowest = flags_ref[0, 2 + i : 3 + i, :]
        bias = bias_row(lowest, [(first + n).astype(jnp.float32) for n in range(i, count)])
        for pair in range(width // LANES):
            cols = slice(pair * LANES, (pair + 1) * LANES)
            total, top, weight = attend(
                qkv_ref[0, rows, cols], keys[i * C :, cols], values[i * C :, cols], bias
            )
            parts = total_ref[rows, cols], top_ref[rows, cols], weight_ref[rows, cols]
            total, _, weight = merged(parts, total, top, weight)
            heads_ref[rows, cols] = (total / weight).astype(jnp.bfloat16)
    window = sent_ref.shape[0]
    other = (1 - lax.axis_index("mp")) * (slab - window)
    sent_ref[...] = jnp.dot(
        heads_ref[pl.ds(pl.multiple_of(other, EDGE), window)],
        w_out_ref[...],
        preferred_element_type=jnp.float32,
    ).astype(jnp.bfloat16)


def base_kernel(heads_ref, w_out_ref, frames_ref, base_ref):
    slab = heads_ref.shape[0]
    window = base_ref.shape[0]
    first = pl.multiple_of(lax.axis_index("mp") * (slab - window), EDGE)
    base_ref[...] = frames_ref[pl.ds(first, window)].astype(jnp.float32) + jnp.dot(
        heads_ref[pl.ds(first, window)], w_out_ref[...], preferred_element_type=jnp.float32
    ).astype(jnp.bfloat16).astype(jnp.float32)


def gate_kernel(
    base_ref, got_ref, gain_ref, w_ref, gated_ref, edge_ref, first_ref, normed, held
):
    window, width = base_ref.shape
    rows = first_ref.shape[0]

    def body(part):
        value = base_ref[part] + got_ref[part].astype(jnp.float32)
        held[part] = value
        normed[part] = norm_rows(value, gain_ref[...]).astype(jnp.bfloat16)

    each(window, 16, body)
    for part in range(0, width, 256):
        cols = slice(part, part + 256)
        value = jnp.dot(normed[...], w_ref[:, cols], preferred_element_type=jnp.float32)
        gate = jnp.dot(
            normed[...],
            w_ref[:, width + part : width + part + 256],
            preferred_element_type=jnp.float32,
        )
        gated_ref[:, cols] = (value * sigmoid(gate)).astype(jnp.bfloat16)
    core = lax.axis_index("mp")
    edge_ref[...] = gated_ref[pl.ds(pl.multiple_of(core * (window - EDGE), EDGE), EDGE)]
    first_ref[...] = held[pl.ds(pl.multiple_of(core * (window - rows), EDGE), rows)]


def conv_kernel(gated_ref, taps_ref, flags_ref, sum_ref, held, padded):
    window, width = gated_ref.shape
    rows = sum_ref.shape[0]
    half = (taps_ref.shape[0] - 1) // 2
    core = lax.axis_index("mp")
    zeros = jnp.zeros((EDGE, width), jnp.float32)
    held[:EDGE] = zeros
    held[rows + EDGE :] = zeros
    held[pl.ds(pl.multiple_of((1 - core) * EDGE, EDGE), window)] = gated_ref[...].astype(
        jnp.float32
    )
    taps = taps_ref[...].astype(jnp.float32)
    for stretch in range(rows // C):
        at = 2 + (rows // C) * core + stretch
        label = flags_ref[1, pl.ds(at, 1), :]
        before = jnp.where(flags_ref[1, pl.ds(at - 1, 1), :] == label, 1.0, 0.0)
        after = jnp.where(flags_ref[1, pl.ds(at + 1, 1), :] == label, 1.0, 0.0)
        low = stretch * C
        for chunk in range(width // LANES):
            cols = slice(chunk * LANES, (chunk + 1) * LANES)
            padded[chunk, :EDGE] = held[low : low + EDGE, cols] * before
            padded[chunk, EDGE : EDGE + C] = held[low + EDGE : low + EDGE + C, cols]
            padded[chunk, EDGE + C :] = held[low + EDGE + C : low + 2 * EDGE + C, cols] * after
        for chunk in range(width // LANES):
            cols = slice(chunk * LANES, (chunk + 1) * LANES)
            for part in range(0, C, 64):
                total = jnp.zeros((64, LANES), jnp.float32)
                for tap in range(taps_ref.shape[0]):
                    at_row = EDGE - half + part + tap
                    total = total + padded[chunk, at_row : at_row + 64] * taps[tap : tap + 1, cols]
                sum_ref[low + part : low + part + 64, cols] = total


def tail_kernel(
    sum_ref, halo_ref, taps_ref, flags_ref, first_ref, gain_depth_ref, gain_ffn_ref, gain_final_ref,
    w_point_ref, up_own_ref, up_other_ref, down_own_ref, down_other_ref,
    out_ref,
    around, depth, normed, second, hidden, feed,
):
    rows, width = sum_ref.shape
    half = (taps_ref.shape[0] - 1) // 2
    units = up_own_ref.shape[1]
    step = 512
    core = lax.axis_index("mp")
    at = 2 + 3 * core
    same = jnp.where(
        flags_ref[1, pl.ds(at, 1), :] == flags_ref[1, pl.ds(at - 1 + 2 * core, 1), :], 1.0, 0.0
    )
    taps = taps_ref[...].astype(jnp.float32)
    depth[...] = sum_ref[...]
    around[...] = jnp.zeros_like(around)
    for chunk in range(width // LANES):
        cols = slice(chunk * LANES, (chunk + 1) * LANES)
        around[chunk, pl.ds(pl.multiple_of(core * 2 * EDGE, EDGE), EDGE)] = (
            halo_ref[:, cols].astype(jnp.float32) * same
        )
    edge = pl.ds(pl.multiple_of(core * (rows - EDGE), EDGE), EDGE)
    for chunk in range(width // LANES):
        cols = slice(chunk * LANES, (chunk + 1) * LANES)
        total = jnp.zeros((EDGE, LANES), jnp.float32)
        for tap in range(taps_ref.shape[0]):
            at_row = EDGE - half + tap
            total = total + around[chunk, at_row : at_row + EDGE] * taps[tap : tap + 1, cols]
        depth[edge, cols] = depth[edge, cols] + total

    def squash(part):
        value = norm_rows(depth[part], gain_depth_ref[...])
        normed[part] = (value * sigmoid(value)).astype(jnp.bfloat16)

    each(rows, 16, squash)
    second[...] = first_ref[...] + jnp.dot(
        normed[...], w_point_ref[...], preferred_element_type=jnp.float32
    )

    def ffn_norm(part):
        normed[part] = norm_rows(second[part], gain_ffn_ref[...]).astype(jnp.bfloat16)

    each(rows, 16, ffn_norm)
    for group, ref in enumerate((up_own_ref, up_other_ref)):
        for part in range(units // step):
            cols = slice(part * step, (part + 1) * step)
            value = jnp.dot(normed[...], ref[:, cols], preferred_element_type=jnp.float32)
            hidden[group, :, cols] = (value * sigmoid(value)).astype(jnp.bfloat16)
    for part in range(width // 256):
        cols = slice(part * 256, (part + 1) * 256)
        total = 0.0
        for group, ref in enumerate((down_own_ref, down_other_ref)):
            total = total + jnp.dot(
                hidden[group], ref[:, cols], preferred_element_type=jnp.float32
            ).astype(jnp.bfloat16).astype(jnp.float32)
        feed[:, cols] = second[:, cols] + 0.5 * total

    def finish(part):
        out_ref[part] = norm_rows(feed[part], gain_final_ref[...]).astype(jnp.bfloat16)

    each(rows, 16, finish)


def on_device(
    frames,
    gain_attn,
    w_qkv,
    w_out,
    gain_conv,
    w_point_in,
    w_depth,
    gain_depth,
    w_point_out,
    gain_ffn,
    w_up,
    w_down,
    gain_final,
    lengths,
    context,
):
    slab, width = frames.shape
    rows = slab // 2
    local = w_qkv.shape[2]
    window = rows + EDGE
    units = w_up.shape[1]
    tm = lax.axis_size("tm")
    bf16, f32 = jnp.bfloat16, jnp.float32
    shape = jax.ShapeDtypeStruct
    swap = [(0, 1), (1, 0)]

    def row(vec):
        return vec.reshape(1, -1)

    w_planes = jnp.transpose(w_qkv, (1, 0, 2))
    sent, normed = pl.pallas_call(
        send_kernel,
        out_shape=(shape((rows, width), bf16), shape((slab, width), bf16)),
        in_specs=[VMEM] * 2,
        out_specs=(VMEM,) * 2,
        compiler_params=params(8),
        cost_estimate=cost(0, 2 * rows * width * 2),
        name="send_norm",
    )(frames, row(gain_attn))
    near_mine = lax.ppermute(sent, "tm", [(i, i + 1) for i in range(tm - 1)])
    qkv, flags = pl.pallas_call(
        own_kernel,
        grid=(3,),
        out_shape=(shape((3, slab, local), bf16), shape((2, 8, LANES), f32)),
        in_specs=[
            pl.BlockSpec((slab, width), lambda i: (0, 0)),
            pl.BlockSpec((1, width, local), lambda i: (i, 0, 0)),
            pl.BlockSpec((1, lengths.shape[0]), lambda i: (0, 0)),
            pl.BlockSpec((1, lengths.shape[0]), lambda i: (0, 0)),
        ],
        out_specs=(
            pl.BlockSpec((1, slab, local), lambda i: (i, 0, 0)),
            pl.BlockSpec((2, 8, LANES), lambda i: (0, 0, 0)),
        ),
        compiler_params=params(16),
        cost_estimate=cost(slab * width * 3 * local, width * 3 * local * 2, EARLY),
        name="own_qkv",
    )(normed, w_planes, row(lengths), row(context))
    partial = (shape((slab, local), f32),) * 3
    own_parts = pl.pallas_call(
        self_kernel,
        out_shape=partial,
        in_specs=[VMEM] * 2,
        out_specs=(VMEM,) * 3,
        compiler_params=params(16),
        cost_estimate=cost(5 * slab * slab * local, 4 * MIB, EARLY),
        name="own_attention",
    )(qkv, flags)
    up_held, down_held, own_parts = lax.optimization_barrier((w_up, w_down, own_parts))
    up_other = lax.ppermute(up_held, "mp", swap)
    down_other = lax.ppermute(down_held, "mp", swap)
    near_mine, own_parts = lax.optimization_barrier((near_mine, own_parts))
    far_mine = lax.ppermute(near_mine, "tm", [(i, i + 1) for i in range(tm - 1)])
    near_theirs = lax.ppermute(near_mine, "mp", swap)
    near_parts = pl.pallas_call(
        near_kernel,
        out_shape=partial,
        in_specs=[VMEM] * 8,
        out_specs=(VMEM,) * 3,
        scratch_shapes=[
            pltpu.VMEM((slab, width), bf16),
            pltpu.VMEM((slab, local), bf16),
            pltpu.VMEM((slab, local), bf16),
        ],
        compiler_params=params(16),
        cost_estimate=cost(slab * width * 2 * local + 8 * slab * slab * local, 8 * MIB, MIDDLE),
        name="near_attention",
    )(qkv, near_mine, near_theirs, w_planes, flags, *own_parts)
    far_mine, near_parts = lax.optimization_barrier((far_mine, near_parts))
    far_theirs = lax.ppermute(far_mine, "mp", swap)
    heads, to_other = pl.pallas_call(
        far_kernel,
        out_shape=(shape((slab, local), bf16), shape((window, width), bf16)),
        in_specs=[VMEM] * 9,
        out_specs=(VMEM,) * 2,
        scratch_shapes=[
            pltpu.VMEM((slab, width), bf16),
            pltpu.VMEM((slab, local), bf16),
            pltpu.VMEM((slab, local), bf16),
        ],
        compiler_params=params(16),
        cost_estimate=cost(slab * width * 2 * local + 3 * slab * slab * local, 10 * MIB, LATE),
        name="far_attention",
    )(qkv, far_mine, far_theirs, w_planes, flags, *near_parts, w_out)
    from_other = lax.ppermute(to_other, "mp", swap)
    base = pl.pallas_call(
        base_kernel,
        out_shape=shape((window, width), f32),
        in_specs=[VMEM] * 3,
        out_specs=VMEM,
        compiler_params=params(12),
        cost_estimate=cost(window * width * local, 3 * MIB, LATE),
        name="out_projection",
    )(heads, w_out, frames)
    gated, edge, first_res = pl.pallas_call(
        gate_kernel,
        out_shape=(
            shape((window, width), bf16),
            shape((EDGE, width), bf16),
            shape((rows, width), f32),
        ),
        in_specs=[VMEM] * 4,
        out_specs=(VMEM,) * 3,
        scratch_shapes=[pltpu.VMEM((window, width), bf16), pltpu.VMEM((window, width), f32)],
        compiler_params=params(16),
        cost_estimate=cost(window * width * 2 * width, 5 * MIB, LATE),
        name="gated_units",
    )(base, from_other, row(gain_conv), w_point_in)
    halo_pairs = [(2 * i + 1, 2 * i + 2) for i in range(tm - 1)]
    halo = lax.ppermute(edge, ("tm", "mp"), halo_pairs + [(b, a) for a, b in halo_pairs])
    depth_sum = pl.pallas_call(
        conv_kernel,
        out_shape=shape((rows, width), f32),
        in_specs=[VMEM] * 3,
        out_specs=VMEM,
        scratch_shapes=[
            pltpu.VMEM((rows + 2 * EDGE, width), f32),
            pltpu.VMEM((width // LANES, C + 2 * EDGE, LANES), f32),
        ],
        compiler_params=params(12),
        cost_estimate=cost(rows * width * 512, MIB, LATE),
        name="depthwise",
    )(gated, w_depth, flags)
    return pl.pallas_call(
        tail_kernel,
        out_shape=shape((rows, width), bf16),
        in_specs=[VMEM] * 13,
        out_specs=VMEM,
        scratch_shapes=[
            pltpu.VMEM((width // LANES, 3 * EDGE, LANES), f32),
            pltpu.VMEM((rows, width), f32),
            pltpu.VMEM((rows, width), bf16),
            pltpu.VMEM((rows, width), f32),
            pltpu.VMEM((2, rows, units), bf16),
            pltpu.VMEM((rows, width), f32),
        ],
        compiler_params=params(12),
        cost_estimate=cost(rows * width * 9 * width, 18 * MIB, LATE),
        name="tail",
    )(
        depth_sum, halo, w_depth, flags, first_res, row(gain_depth), row(gain_ffn),
        row(gain_final), w_point_out, w_up, up_other, w_down, down_other,
    )


def solution(mesh):
    in_specs = (
        P("tm", None),
        P(),
        P(None, None, "mp"),
        P("mp", None),
        P(),
        P(),
        P(),
        P(),
        P(),
        P(),
        P(None, "mp"),
        P("mp", None),
        P(),
        P(),
        P(),
    )
    out_specs = P(("tm", "mp"), None)
    return jax.shard_map(
        on_device, mesh=mesh, in_specs=in_specs, out_specs=out_specs, check_vma=False
    )
```

```python
import jax
import jax.numpy as jnp
from jax import lax
from jax.experimental import pallas as pl
from jax.experimental.pallas import tpu as pltpu
from jax.sharding import PartitionSpec as P

HD = 64
C = 128
LANES = 128
EPSILON = 1e-05
NEGATIVE = -1e30
EDGE = 16
MIB = 1 << 20
EARLY = 0.001
LATE = 8.0
MIDDLE = 1.0
VMEM = pl.BlockSpec(memory_space=pltpu.VMEM)
HBM = pl.BlockSpec(memory_space=pltpu.HBM)


def params(limit):
    return pltpu.CompilerParams(vmem_limit_bytes=limit * MIB)


def cost(macs, read, share=1.0):
    return pl.CostEstimate(
        flops=int(2 * macs * share), bytes_accessed=int(read * share), transcendentals=0
    )


def norm_rows(values, gain):
    centred = values - jnp.mean(values, axis=-1, keepdims=True)
    variance = jnp.mean(centred * centred, axis=-1, keepdims=True)
    return centred * lax.rsqrt(variance + EPSILON) * gain


def sigmoid(values):
    return 0.5 + 0.5 * jnp.tanh(0.5 * values)


def each(rows, step, body):
    for first in range(0, rows, step):
        body(slice(first, first + step))


def send_kernel(frames_ref, gain_ref, sent_ref, normed_ref):
    rows = sent_ref.shape[0]

    def body(part):
        normed_ref[part] = norm_rows(
            frames_ref[part].astype(jnp.float32), gain_ref[...]
        ).astype(jnp.bfloat16)

    each(normed_ref.shape[0], 16, body)
    first = pl.multiple_of(lax.axis_index("mp") * rows, rows)
    sent_ref[...] = normed_ref[pl.ds(first, rows)]


def own_kernel(normed_ref, w_ref, lengths_ref, context_ref, qkv_ref, flags_ref):
    rows = normed_ref.shape[0]
    step = pl.program_id(0)

    @pl.when(step == 0)
    def _():
        count = lengths_ref.shape[1]
        lengths = jnp.broadcast_to(lengths_ref[...], (8, count))
        before = (
            lax.broadcasted_iota(jnp.int32, (count, count), 0)
            < lax.broadcasted_iota(jnp.int32, (count, count), 1)
        ).astype(jnp.float32).astype(jnp.bfloat16)
        start = jnp.dot(
            lengths.astype(jnp.float32).astype(jnp.bfloat16),
            before,
            preferred_element_type=jnp.float32,
        )
        stretch = (
            lax.axis_index("tm") * (rows // C)
            - 2
            + lax.broadcasted_iota(jnp.int32, (8, count), 0)
        ).astype(jnp.float32)
        end = start + lengths.astype(jnp.float32)
        member = jnp.where((start <= stretch) & (stretch < end), 1.0, 0.0)
        context = jnp.broadcast_to(context_ref[...], (8, count)).astype(jnp.float32)
        number = lax.broadcasted_iota(jnp.int32, (8, count), 1).astype(jnp.float32) + 1.0
        opening = jnp.sum(member * start, axis=1, keepdims=True)
        reached = jnp.sum(member * context, axis=1, keepdims=True)
        label = jnp.sum(member * number, axis=1, keepdims=True)
        flags_ref[0] = jnp.maximum(stretch[:, :LANES] - reached, opening)
        flags_ref[1] = jnp.broadcast_to(label, (8, LANES))

    scale = jnp.where(step == 0, HD**-0.5, 1.0)
    qkv_ref[0] = (
        jnp.dot(normed_ref[...], w_ref[0], preferred_element_type=jnp.float32) * scale
    ).astype(jnp.bfloat16)


def bias_row(lowest, stretches):
    return jnp.concatenate(
        [jnp.where(stretch >= lowest, 0.0, NEGATIVE) for stretch in stretches], axis=1
    )


def attend_all(queries, keys, values, biases):
    first_head = lax.broadcasted_iota(jnp.int32, (C, LANES), 1) < HD
    zero = jnp.zeros_like(queries[0])
    stacked = []
    for query in queries:
        stacked += [jnp.where(first_head, query, zero), jnp.where(first_head, zero, query)]
    scores = lax.dot_general(
        jnp.concatenate(stacked, axis=0),
        keys,
        (((1,), (1,)), ((), ())),
        preferred_element_type=jnp.float32,
    )
    raised, tops = [], []
    for i, bias in enumerate(biases):
        part = scores[2 * i * C : 2 * (i + 1) * C] + bias
        highest = jnp.max(part, axis=1, keepdims=True)
        raised.append(jnp.exp(part - highest).astype(jnp.bfloat16))
        tops.append(highest)
    wide = jnp.concatenate([values, jnp.ones_like(values)], axis=1)
    mixed = jnp.dot(jnp.concatenate(raised, axis=0), wide, preferred_element_type=jnp.float32)
    found = []
    for i, highest in enumerate(tops):
        one = mixed[2 * i * C : (2 * i + 1) * C]
        two = mixed[(2 * i + 1) * C : 2 * (i + 1) * C]
        total = jnp.where(first_head, one[:, :LANES], two[:, :LANES])
        weight = jnp.where(first_head, one[:, LANES:], two[:, LANES:])
        top = jnp.where(
            first_head,
            jnp.broadcast_to(highest[:C], (C, LANES)),
            jnp.broadcast_to(highest[C:], (C, LANES)),
        )
        found.append((total, top, weight))
    return found


def attend(query, keys, values, bias):
    return attend_all([query], keys, values, [bias])[0]


def place(normed, mine_ref, theirs_ref):
    rows = mine_ref.shape[0]
    core = lax.axis_index("mp")
    normed[pl.ds(pl.multiple_of(core * rows, rows), rows)] = mine_ref[...]
    normed[pl.ds(pl.multiple_of((1 - core) * rows, rows), rows)] = theirs_ref[...]


def merged(parts, total, top, weight):
    other_total, other_top, other_weight = parts
    highest = jnp.maximum(other_top, top)
    other_part = jnp.exp(other_top - highest)
    part = jnp.exp(top - highest)
    return (
        other_total * other_part + total * part,
        highest,
        other_weight * other_part + weight * part,
    )


def self_kernel(qkv_ref, flags_ref, total_ref, top_ref, weight_ref):
    slab, width = qkv_ref.shape[1:]
    count = slab // C
    first = lax.axis_index("tm") * count
    for i in range(count):
        rows = slice(i * C, (i + 1) * C)
        lowest = flags_ref[0, 2 + i : 3 + i, :]
        bias = bias_row(lowest, [(first + n).astype(jnp.float32) for n in range(i + 1)])
        for pair in range(width // LANES):
            cols = slice(pair * LANES, (pair + 1) * LANES)
            seen = slice(0, (i + 1) * C)
            total_ref[rows, cols], top_ref[rows, cols], weight_ref[rows, cols] = attend(
                qkv_ref[0, rows, cols], qkv_ref[1, seen, cols], qkv_ref[2, seen, cols], bias
            )


def near_kernel(
    qkv_ref, mine_ref, theirs_ref, w_ref, flags_ref, own_total_ref, own_top_ref, own_weight_ref,
    total_ref, top_ref, weight_ref,
    normed, keys, values,
):
    slab, width = qkv_ref.shape[1:]
    count = slab // C
    place(normed, mine_ref, theirs_ref)
    keys[...] = jnp.dot(normed[...], w_ref[1], preferred_element_type=jnp.float32).astype(
        jnp.bfloat16
    )
    values[...] = jnp.dot(normed[...], w_ref[2], preferred_element_type=jnp.float32).astype(
        jnp.bfloat16
    )
    first = lax.axis_index("tm") * count - count
    every = [slice(i * C, (i + 1) * C) for i in range(count)]
    seen = [(first + n).astype(jnp.float32) for n in range(count)]
    biases = [bias_row(flags_ref[0, 2 + i : 3 + i, :], seen) for i in range(count)]
    for pair in range(width // LANES):
        cols = slice(pair * LANES, (pair + 1) * LANES)
        found = attend_all(
            [qkv_ref[0, rows, cols] for rows in every], keys[:, cols], values[:, cols], biases
        )
        for rows, part in zip(every, found):
            parts = own_total_ref[rows, cols], own_top_ref[rows, cols], own_weight_ref[rows, cols]
            total_ref[rows, cols], top_ref[rows, cols], weight_ref[rows, cols] = merged(
                parts, *part
            )


def far_kernel(
    qkv_ref, mine_ref, theirs_ref, w_ref, flags_ref, total_ref, top_ref, weight_ref, w_out_ref,
    heads_ref, sent_ref, normed, keys, values,
):
    slab, width = qkv_ref.shape[1:]
    count = slab // C
    place(normed, mine_ref, theirs_ref)
    keys[...] = jnp.dot(normed[...], w_ref[1], preferred_element_type=jnp.float32).astype(
        jnp.bfloat16
    )
    values[...] = jnp.dot(normed[...], w_ref[2], preferred_element_type=jnp.float32).astype(
        jnp.bfloat16
    )
    first = lax.axis_index("tm") * count - 2 * count
    for i in range(count):
        rows = slice(i * C, (i + 1) * C)
        lowest = flags_ref[0, 2 + i : 3 + i, :]
        bias = bias_row(lowest, [(first + n).astype(jnp.float32) for n in range(i, count)])
        for pair in range(width // LANES):
            cols = slice(pair * LANES, (pair + 1) * LANES)
            total, top, weight = attend(
                qkv_ref[0, rows, cols], keys[i * C :, cols], values[i * C :, cols], bias
            )
            parts = total_ref[rows, cols], top_ref[rows, cols], weight_ref[rows, cols]
            total, _, weight = merged(parts, total, top, weight)
            heads_ref[rows, cols] = (total / weight).astype(jnp.bfloat16)
    window = sent_ref.shape[0]
    other = (1 - lax.axis_index("mp")) * (slab - window)
    sent_ref[...] = jnp.dot(
        heads_ref[pl.ds(pl.multiple_of(other, EDGE), window)],
        w_out_ref[...],
        preferred_element_type=jnp.float32,
    ).astype(jnp.bfloat16)


def base_kernel(heads_ref, w_out_ref, frames_ref, base_ref):
    slab = heads_ref.shape[0]
    window = base_ref.shape[0]
    first = pl.multiple_of(lax.axis_index("mp") * (slab - window), EDGE)
    base_ref[...] = frames_ref[pl.ds(first, window)].astype(jnp.float32) + jnp.dot(
        heads_ref[pl.ds(first, window)], w_out_ref[...], preferred_element_type=jnp.float32
    ).astype(jnp.bfloat16).astype(jnp.float32)


def gate_kernel(
    base_ref, got_ref, gain_ref, w_ref, gated_ref, edge_ref, first_ref, normed, held
):
    window, width = base_ref.shape
    rows = first_ref.shape[0]

    def body(part):
        value = base_ref[part] + got_ref[part].astype(jnp.float32)
        held[part] = value
        normed[part] = norm_rows(value, gain_ref[...]).astype(jnp.bfloat16)

    each(window, 16, body)
    for part in range(0, width, 256):
        cols = slice(part, part + 256)
        value = jnp.dot(normed[...], w_ref[:, cols], preferred_element_type=jnp.float32)
        gate = jnp.dot(
            normed[...],
            w_ref[:, width + part : width + part + 256],
            preferred_element_type=jnp.float32,
        )
        gated_ref[:, cols] = (value * sigmoid(gate)).astype(jnp.bfloat16)
    core = lax.axis_index("mp")
    edge_ref[...] = gated_ref[pl.ds(pl.multiple_of(core * (window - EDGE), EDGE), EDGE)]
    first_ref[...] = held[pl.ds(pl.multiple_of(core * (window - rows), EDGE), rows)]


def conv_kernel(gated_ref, taps_ref, flags_ref, sum_ref, held, padded):
    window, width = gated_ref.shape
    rows = sum_ref.shape[0]
    half = (taps_ref.shape[0] - 1) // 2
    core = lax.axis_index("mp")
    zeros = jnp.zeros((EDGE, width), jnp.float32)
    held[:EDGE] = zeros
    held[rows + EDGE :] = zeros
    held[pl.ds(pl.multiple_of((1 - core) * EDGE, EDGE), window)] = gated_ref[...].astype(
        jnp.float32
    )
    taps = taps_ref[...].astype(jnp.float32)
    for stretch in range(rows // C):
        at = 2 + (rows // C) * core + stretch
        label = flags_ref[1, pl.ds(at, 1), :]
        before = jnp.where(flags_ref[1, pl.ds(at - 1, 1), :] == label, 1.0, 0.0)
        after = jnp.where(flags_ref[1, pl.ds(at + 1, 1), :] == label, 1.0, 0.0)
        low = stretch * C
        for chunk in range(width // LANES):
            cols = slice(chunk * LANES, (chunk + 1) * LANES)
            padded[chunk, :EDGE] = held[low : low + EDGE, cols] * before
            padded[chunk, EDGE : EDGE + C] = held[low + EDGE : low + EDGE + C, cols]
            padded[chunk, EDGE + C :] = held[low + EDGE + C : low + 2 * EDGE + C, cols] * after
        for chunk in range(width // LANES):
            cols = slice(chunk * LANES, (chunk + 1) * LANES)
            for part in range(0, C, 64):
                total = jnp.zeros((64, LANES), jnp.float32)
                for tap in range(taps_ref.shape[0]):
                    at_row = EDGE - half + part + tap
                    total = total + padded[chunk, at_row : at_row + 64] * taps[tap : tap + 1, cols]
                sum_ref[low + part : low + part + 64, cols] = total


def tail_kernel(
    sum_ref, halo_ref, taps_ref, flags_ref, first_ref, gain_depth_ref, gain_ffn_ref, gain_final_ref,
    w_point_ref, up_own_ref, up_other_ref, down_own_ref, down_other_ref,
    out_ref,
    around, depth, normed, second, hidden, feed,
):
    rows, width = sum_ref.shape
    half = (taps_ref.shape[0] - 1) // 2
    units = up_own_ref.shape[1]
    step = 512
    core = lax.axis_index("mp")
    at = 2 + 3 * core
    same = jnp.where(
        flags_ref[1, pl.ds(at, 1), :] == flags_ref[1, pl.ds(at - 1 + 2 * core, 1), :], 1.0, 0.0
    )
    taps = taps_ref[...].astype(jnp.float32)
    depth[...] = sum_ref[...]
    around[...] = jnp.zeros_like(around)
    for chunk in range(width // LANES):
        cols = slice(chunk * LANES, (chunk + 1) * LANES)
        around[chunk, pl.ds(pl.multiple_of(core * 2 * EDGE, EDGE), EDGE)] = (
            halo_ref[:, cols].astype(jnp.float32) * same
        )
    edge = pl.ds(pl.multiple_of(core * (rows - EDGE), EDGE), EDGE)
    for chunk in range(width // LANES):
        cols = slice(chunk * LANES, (chunk + 1) * LANES)
        total = jnp.zeros((EDGE, LANES), jnp.float32)
        for tap in range(taps_ref.shape[0]):
            at_row = EDGE - half + tap
            total = total + around[chunk, at_row : at_row + EDGE] * taps[tap : tap + 1, cols]
        depth[edge, cols] = depth[edge, cols] + total

    def squash(part):
        value = norm_rows(depth[part], gain_depth_ref[...])
        normed[part] = (value * sigmoid(value)).astype(jnp.bfloat16)

    each(rows, 16, squash)
    second[...] = first_ref[...] + jnp.dot(
        normed[...], w_point_ref[...], preferred_element_type=jnp.float32
    )

    def ffn_norm(part):
        normed[part] = norm_rows(second[part], gain_ffn_ref[...]).astype(jnp.bfloat16)

    each(rows, 16, ffn_norm)
    for group, ref in enumerate((up_own_ref, up_other_ref)):
        for part in range(units // step):
            cols = slice(part * step, (part + 1) * step)
            value = jnp.dot(normed[...], ref[:, cols], preferred_element_type=jnp.float32)
            hidden[group, :, cols] = (value * sigmoid(value)).astype(jnp.bfloat16)
    for part in range(width // 256):
        cols = slice(part * 256, (part + 1) * 256)
        total = 0.0
        for group, ref in enumerate((down_own_ref, down_other_ref)):
            total = total + jnp.dot(
                hidden[group], ref[:, cols], preferred_element_type=jnp.float32
            ).astype(jnp.bfloat16).astype(jnp.float32)
        feed[:, cols] = second[:, cols] + 0.5 * total

    def finish(part):
        out_ref[part] = norm_rows(feed[part], gain_final_ref[...]).astype(jnp.bfloat16)

    each(rows, 16, finish)


def on_device(
    frames,
    gain_attn,
    w_qkv,
    w_out,
    gain_conv,
    w_point_in,
    w_depth,
    gain_depth,
    w_point_out,
    gain_ffn,
    w_up,
    w_down,
    gain_final,
    lengths,
    context,
):
    slab, width = frames.shape
    rows = slab // 2
    local = w_qkv.shape[2]
    window = rows + EDGE
    units = w_up.shape[1]
    tm = lax.axis_size("tm")
    bf16, f32 = jnp.bfloat16, jnp.float32
    shape = jax.ShapeDtypeStruct
    swap = [(0, 1), (1, 0)]

    def row(vec):
        return vec.reshape(1, -1)

    w_planes = jnp.transpose(w_qkv, (1, 0, 2))
    sent, normed = pl.pallas_call(
        send_kernel,
        out_shape=(shape((rows, width), bf16), shape((slab, width), bf16)),
        in_specs=[VMEM] * 2,
        out_specs=(VMEM,) * 2,
        compiler_params=params(8),
        cost_estimate=cost(0, 2 * rows * width * 2),
        name="send_norm",
    )(frames, row(gain_attn))
    near_mine = lax.ppermute(sent, "tm", [(i, i + 1) for i in range(tm - 1)])
    far_mine = lax.ppermute(sent, "tm", [(i, i + 2) for i in range(tm - 2)])
    qkv, flags = pl.pallas_call(
        own_kernel,
        grid=(3,),
        out_shape=(shape((3, slab, local), bf16), shape((2, 8, LANES), f32)),
        in_specs=[
            pl.BlockSpec((slab, width), lambda i: (0, 0)),
            pl.BlockSpec((1, width, local), lambda i: (i, 0, 0)),
            pl.BlockSpec((1, lengths.shape[0]), lambda i: (0, 0)),
            pl.BlockSpec((1, lengths.shape[0]), lambda i: (0, 0)),
        ],
        out_specs=(
            pl.BlockSpec((1, slab, local), lambda i: (i, 0, 0)),
            pl.BlockSpec((2, 8, LANES), lambda i: (0, 0, 0)),
        ),
        compiler_params=params(16),
        cost_estimate=cost(slab * width * 3 * local, width * 3 * local * 2, EARLY),
        name="own_qkv",
    )(normed, w_planes, row(lengths), row(context))
    partial = (shape((slab, local), f32),) * 3
    own_parts = pl.pallas_call(
        self_kernel,
        out_shape=partial,
        in_specs=[VMEM] * 2,
        out_specs=(VMEM,) * 3,
        compiler_params=params(16),
        cost_estimate=cost(5 * slab * slab * local, 4 * MIB, EARLY),
        name="own_attention",
    )(qkv, flags)
    up_held, down_held, own_parts = lax.optimization_barrier((w_up, w_down, own_parts))
    up_other = lax.ppermute(up_held, "mp", swap)
    down_other = lax.ppermute(down_held, "mp", swap)
    near_mine, far_mine, own_parts = lax.optimization_barrier((near_mine, far_mine, own_parts))
    near_theirs = lax.ppermute(near_mine, "mp", swap)
    near_parts = pl.pallas_call(
        near_kernel,
        out_shape=partial,
        in_specs=[VMEM] * 8,
        out_specs=(VMEM,) * 3,
        scratch_shapes=[
            pltpu.VMEM((slab, width), bf16),
            pltpu.VMEM((slab, local), bf16),
            pltpu.VMEM((slab, local), bf16),
        ],
        compiler_params=params(16),
        cost_estimate=cost(slab * width * 2 * local + 8 * slab * slab * local, 8 * MIB, MIDDLE),
        name="near_attention",
    )(qkv, near_mine, near_theirs, w_planes, flags, *own_parts)
    far_theirs = lax.ppermute(far_mine, "mp", swap)
    heads, to_other = pl.pallas_call(
        far_kernel,
        out_shape=(shape((slab, local), bf16), shape((window, width), bf16)),
        in_specs=[VMEM] * 9,
        out_specs=(VMEM,) * 2,
        scratch_shapes=[
            pltpu.VMEM((slab, width), bf16),
            pltpu.VMEM((slab, local), bf16),
            pltpu.VMEM((slab, local), bf16),
        ],
        compiler_params=params(16),
        cost_estimate=cost(slab * width * 2 * local + 3 * slab * slab * local, 10 * MIB, LATE),
        name="far_attention",
    )(qkv, far_mine, far_theirs, w_planes, flags, *near_parts, w_out)
    from_other = lax.ppermute(to_other, "mp", swap)
    base = pl.pallas_call(
        base_kernel,
        out_shape=shape((window, width), f32),
        in_specs=[VMEM] * 3,
        out_specs=VMEM,
        compiler_params=params(12),
        cost_estimate=cost(window * width * local, 3 * MIB, LATE),
        name="out_projection",
    )(heads, w_out, frames)
    gated, edge, first_res = pl.pallas_call(
        gate_kernel,
        out_shape=(
            shape((window, width), bf16),
            shape((EDGE, width), bf16),
            shape((rows, width), f32),
        ),
        in_specs=[VMEM] * 4,
        out_specs=(VMEM,) * 3,
        scratch_shapes=[pltpu.VMEM((window, width), bf16), pltpu.VMEM((window, width), f32)],
        compiler_params=params(16),
        cost_estimate=cost(window * width * 2 * width, 5 * MIB, LATE),
        name="gated_units",
    )(base, from_other, row(gain_conv), w_point_in)
    halo_pairs = [(2 * i + 1, 2 * i + 2) for i in range(tm - 1)]
    halo = lax.ppermute(edge, ("tm", "mp"), halo_pairs + [(b, a) for a, b in halo_pairs])
    depth_sum = pl.pallas_call(
        conv_kernel,
        out_shape=shape((rows, width), f32),
        in_specs=[VMEM] * 3,
        out_specs=VMEM,
        scratch_shapes=[
            pltpu.VMEM((rows + 2 * EDGE, width), f32),
            pltpu.VMEM((width // LANES, C + 2 * EDGE, LANES), f32),
        ],
        compiler_params=params(12),
        cost_estimate=cost(rows * width * 512, MIB, LATE),
        name="depthwise",
    )(gated, w_depth, flags)
    return pl.pallas_call(
        tail_kernel,
        out_shape=shape((rows, width), bf16),
        in_specs=[VMEM] * 13,
        out_specs=VMEM,
        scratch_shapes=[
            pltpu.VMEM((width // LANES, 3 * EDGE, LANES), f32),
            pltpu.VMEM((rows, width), f32),
            pltpu.VMEM((rows, width), bf16),
            pltpu.VMEM((rows, width), f32),
            pltpu.VMEM((2, rows, units), bf16),
            pltpu.VMEM((rows, width), f32),
        ],
        compiler_params=params(12),
        cost_estimate=cost(rows * width * 9 * width, 18 * MIB, LATE),
        name="tail",
    )(
        depth_sum, halo, w_depth, flags, first_res, row(gain_depth), row(gain_ffn),
        row(gain_final), w_point_out, w_up, up_other, w_down, down_other,
    )


def solution(mesh):
    in_specs = (
        P("tm", None),
        P(),
        P(None, None, "mp"),
        P("mp", None),
        P(),
        P(),
        P(),
        P(),
        P(),
        P(),
        P(None, "mp"),
        P("mp", None),
        P(),
        P(),
        P(),
    )
    out_specs = P(("tm", "mp"), None)
    return jax.shard_map(
        on_device, mesh=mesh, in_specs=in_specs, out_specs=out_specs, check_vma=False
    )
```

```python
import jax
import jax.numpy as jnp
from jax import lax
from jax.experimental import pallas as pl
from jax.experimental.pallas import tpu as pltpu
from jax.sharding import PartitionSpec as P

HD = 64
C = 128
LANES = 128
EPSILON = 1e-05
NEGATIVE = -1e30
EDGE = 16
MIB = 1 << 20
EARLY = 0.001
LATE = 14.5
MIDDLE = 0.1
VMEM = pl.BlockSpec(memory_space=pltpu.VMEM)
HBM = pl.BlockSpec(memory_space=pltpu.HBM)


def params(limit):
    return pltpu.CompilerParams(vmem_limit_bytes=limit * MIB)


def cost(macs, read, share=1.0):
    return pl.CostEstimate(
        flops=int(2 * macs * share), bytes_accessed=int(read * share), transcendentals=0
    )


def norm_rows(values, gain):
    centred = values - jnp.mean(values, axis=-1, keepdims=True)
    variance = jnp.mean(centred * centred, axis=-1, keepdims=True)
    return centred * lax.rsqrt(variance + EPSILON) * gain


def sigmoid(values):
    return 0.5 + 0.5 * jnp.tanh(0.5 * values)


def each(rows, step, body):
    for first in range(0, rows, step):
        body(slice(first, first + step))


def send_kernel(frames_ref, gain_ref, sent_ref, normed_ref):
    rows = sent_ref.shape[0]

    def body(part):
        normed_ref[part] = norm_rows(
            frames_ref[part].astype(jnp.float32), gain_ref[...]
        ).astype(jnp.bfloat16)

    each(normed_ref.shape[0], 16, body)
    first = pl.multiple_of(lax.axis_index("mp") * rows, rows)
    sent_ref[...] = normed_ref[pl.ds(first, rows)]


def own_kernel(normed_ref, w_ref, lengths_ref, context_ref, qkv_ref, flags_ref):
    rows = normed_ref.shape[0]
    step = pl.program_id(0)

    @pl.when(step == 0)
    def _():
        count = lengths_ref.shape[1]
        lengths = jnp.broadcast_to(lengths_ref[...], (8, count))
        before = (
            lax.broadcasted_iota(jnp.int32, (count, count), 0)
            < lax.broadcasted_iota(jnp.int32, (count, count), 1)
        ).astype(jnp.float32).astype(jnp.bfloat16)
        start = jnp.dot(
            lengths.astype(jnp.float32).astype(jnp.bfloat16),
            before,
            preferred_element_type=jnp.float32,
        )
        stretch = (
            lax.axis_index("tm") * (rows // C)
            - 2
            + lax.broadcasted_iota(jnp.int32, (8, count), 0)
        ).astype(jnp.float32)
        end = start + lengths.astype(jnp.float32)
        member = jnp.where((start <= stretch) & (stretch < end), 1.0, 0.0)
        context = jnp.broadcast_to(context_ref[...], (8, count)).astype(jnp.float32)
        number = lax.broadcasted_iota(jnp.int32, (8, count), 1).astype(jnp.float32) + 1.0
        opening = jnp.sum(member * start, axis=1, keepdims=True)
        reached = jnp.sum(member * context, axis=1, keepdims=True)
        label = jnp.sum(member * number, axis=1, keepdims=True)
        flags_ref[0] = jnp.maximum(stretch[:, :LANES] - reached, opening)
        flags_ref[1] = jnp.broadcast_to(label, (8, LANES))

    scale = jnp.where(step == 0, HD**-0.5, 1.0)
    qkv_ref[0] = (
        jnp.dot(normed_ref[...], w_ref[0], preferred_element_type=jnp.float32) * scale
    ).astype(jnp.bfloat16)


def bias_row(lowest, stretches):
    return jnp.concatenate(
        [jnp.where(stretch >= lowest, 0.0, NEGATIVE) for stretch in stretches], axis=1
    )


def attend_all(queries, keys, values, biases):
    first_head = lax.broadcasted_iota(jnp.int32, (C, LANES), 1) < HD
    zero = jnp.zeros_like(queries[0])
    stacked = []
    for query in queries:
        stacked += [jnp.where(first_head, query, zero), jnp.where(first_head, zero, query)]
    scores = lax.dot_general(
        jnp.concatenate(stacked, axis=0),
        keys,
        (((1,), (1,)), ((), ())),
        preferred_element_type=jnp.float32,
    )
    raised, tops = [], []
    for i, bias in enumerate(biases):
        part = scores[2 * i * C : 2 * (i + 1) * C] + bias
        highest = jnp.max(part, axis=1, keepdims=True)
        raised.append(jnp.exp(part - highest).astype(jnp.bfloat16))
        tops.append(highest)
    wide = jnp.concatenate([values, jnp.ones_like(values)], axis=1)
    mixed = jnp.dot(jnp.concatenate(raised, axis=0), wide, preferred_element_type=jnp.float32)
    found = []
    for i, highest in enumerate(tops):
        one = mixed[2 * i * C : (2 * i + 1) * C]
        two = mixed[(2 * i + 1) * C : 2 * (i + 1) * C]
        total = jnp.where(first_head, one[:, :LANES], two[:, :LANES])
        weight = jnp.where(first_head, one[:, LANES:], two[:, LANES:])
        top = jnp.where(
            first_head,
            jnp.broadcast_to(highest[:C], (C, LANES)),
            jnp.broadcast_to(highest[C:], (C, LANES)),
        )
        found.append((total, top, weight))
    return found


def attend(query, keys, values, bias):
    return attend_all([query], keys, values, [bias])[0]


def place(normed, mine_ref, *theirs_refs):
    rows = mine_ref.shape[0]
    core = lax.axis_index("mp")
    normed[pl.ds(pl.multiple_of(core * rows, rows), rows)] = mine_ref[...]
    first = pl.multiple_of((1 - core) * rows, rows)
    for ref in theirs_refs:
        normed[pl.ds(first, ref.shape[0])] = ref[...]
        first = pl.multiple_of(first + ref.shape[0], EDGE)


def merged(parts, total, top, weight):
    other_total, other_top, other_weight = parts
    highest = jnp.maximum(other_top, top)
    other_part = jnp.exp(other_top - highest)
    part = jnp.exp(top - highest)
    return (
        other_total * other_part + total * part,
        highest,
        other_weight * other_part + weight * part,
    )


def self_kernel(qkv_ref, flags_ref, total_ref, top_ref, weight_ref):
    slab, width = qkv_ref.shape[1:]
    count = slab // C
    first = lax.axis_index("tm") * count
    for i in range(count):
        rows = slice(i * C, (i + 1) * C)
        lowest = flags_ref[0, 2 + i : 3 + i, :]
        bias = bias_row(lowest, [(first + n).astype(jnp.float32) for n in range(i + 1)])
        for pair in range(width // LANES):
            cols = slice(pair * LANES, (pair + 1) * LANES)
            seen = slice(0, (i + 1) * C)
            total_ref[rows, cols], top_ref[rows, cols], weight_ref[rows, cols] = attend(
                qkv_ref[0, rows, cols], qkv_ref[1, seen, cols], qkv_ref[2, seen, cols], bias
            )


def near_kernel(
    qkv_ref, mine_ref, first_ref, second_ref, w_ref, flags_ref,
    own_total_ref, own_top_ref, own_weight_ref,
    total_ref, top_ref, weight_ref,
    normed, keys, values,
):
    slab, width = qkv_ref.shape[1:]
    count = slab // C
    place(normed, mine_ref, first_ref, second_ref)
    keys[...] = jnp.dot(normed[...], w_ref[1], preferred_element_type=jnp.float32).astype(
        jnp.bfloat16
    )
    values[...] = jnp.dot(normed[...], w_ref[2], preferred_element_type=jnp.float32).astype(
        jnp.bfloat16
    )
    first = lax.axis_index("tm") * count - count
    every = [slice(i * C, (i + 1) * C) for i in range(count)]
    seen = [(first + n).astype(jnp.float32) for n in range(count)]
    biases = [bias_row(flags_ref[0, 2 + i : 3 + i, :], seen) for i in range(count)]
    for pair in range(width // LANES):
        cols = slice(pair * LANES, (pair + 1) * LANES)
        found = attend_all(
            [qkv_ref[0, rows, cols] for rows in every], keys[:, cols], values[:, cols], biases
        )
        for rows, part in zip(every, found):
            parts = own_total_ref[rows, cols], own_top_ref[rows, cols], own_weight_ref[rows, cols]
            total_ref[rows, cols], top_ref[rows, cols], weight_ref[rows, cols] = merged(
                parts, *part
            )


def far_kernel(
    qkv_ref, mine_ref, theirs_ref, w_ref, flags_ref, total_ref, top_ref, weight_ref, w_out_ref,
    heads_ref, sent_ref, normed, keys, values,
):
    slab, width = qkv_ref.shape[1:]
    count = slab // C
    place(normed, mine_ref, theirs_ref)
    keys[...] = jnp.dot(normed[...], w_ref[1], preferred_element_type=jnp.float32).astype(
        jnp.bfloat16
    )
    values[...] = jnp.dot(normed[...], w_ref[2], preferred_element_type=jnp.float32).astype(
        jnp.bfloat16
    )
    first = lax.axis_index("tm") * count - 2 * count
    for i in range(count):
        rows = slice(i * C, (i + 1) * C)
        lowest = flags_ref[0, 2 + i : 3 + i, :]
        bias = bias_row(lowest, [(first + n).astype(jnp.float32) for n in range(i, count)])
        for pair in range(width // LANES):
            cols = slice(pair * LANES, (pair + 1) * LANES)
            total, top, weight = attend(
                qkv_ref[0, rows, cols], keys[i * C :, cols], values[i * C :, cols], bias
            )
            parts = total_ref[rows, cols], top_ref[rows, cols], weight_ref[rows, cols]
            total, _, weight = merged(parts, total, top, weight)
            heads_ref[rows, cols] = (total / weight).astype(jnp.bfloat16)
    window = sent_ref.shape[0]
    other = (1 - lax.axis_index("mp")) * (slab - window)
    sent_ref[...] = jnp.dot(
        heads_ref[pl.ds(pl.multiple_of(other, EDGE), window)],
        w_out_ref[...],
        preferred_element_type=jnp.float32,
    ).astype(jnp.bfloat16)


def base_kernel(heads_ref, w_out_ref, frames_ref, base_ref):
    slab = heads_ref.shape[0]
    window = base_ref.shape[0]
    first = pl.multiple_of(lax.axis_index("mp") * (slab - window), EDGE)
    base_ref[...] = frames_ref[pl.ds(first, window)].astype(jnp.float32) + jnp.dot(
        heads_ref[pl.ds(first, window)], w_out_ref[...], preferred_element_type=jnp.float32
    ).astype(jnp.bfloat16).astype(jnp.float32)


def gate_kernel(
    base_ref, got_ref, gain_ref, w_ref, gated_ref, edge_ref, first_ref, normed, held
):
    window, width = base_ref.shape
    rows = first_ref.shape[0]

    def body(part):
        value = base_ref[part] + got_ref[part].astype(jnp.float32)
        held[part] = value
        normed[part] = norm_rows(value, gain_ref[...]).astype(jnp.bfloat16)

    each(window, 16, body)
    for part in range(0, width, 256):
        cols = slice(part, part + 256)
        value = jnp.dot(normed[...], w_ref[:, cols], preferred_element_type=jnp.float32)
        gate = jnp.dot(
            normed[...],
            w_ref[:, width + part : width + part + 256],
            preferred_element_type=jnp.float32,
        )
        gated_ref[:, cols] = (value * sigmoid(gate)).astype(jnp.bfloat16)
    core = lax.axis_index("mp")
    edge_ref[...] = gated_ref[pl.ds(pl.multiple_of(core * (window - EDGE), EDGE), EDGE)]
    first_ref[...] = held[pl.ds(pl.multiple_of(core * (window - rows), EDGE), rows)]


def conv_kernel(gated_ref, taps_ref, flags_ref, sum_ref, held, padded):
    window, width = gated_ref.shape
    rows = sum_ref.shape[0]
    half = (taps_ref.shape[0] - 1) // 2
    core = lax.axis_index("mp")
    zeros = jnp.zeros((EDGE, width), jnp.float32)
    held[:EDGE] = zeros
    held[rows + EDGE :] = zeros
    held[pl.ds(pl.multiple_of((1 - core) * EDGE, EDGE), window)] = gated_ref[...].astype(
        jnp.float32
    )
    taps = taps_ref[...].astype(jnp.float32)
    for stretch in range(rows // C):
        at = 2 + (rows // C) * core + stretch
        label = flags_ref[1, pl.ds(at, 1), :]
        before = jnp.where(flags_ref[1, pl.ds(at - 1, 1), :] == label, 1.0, 0.0)
        after = jnp.where(flags_ref[1, pl.ds(at + 1, 1), :] == label, 1.0, 0.0)
        low = stretch * C
        for chunk in range(width // LANES):
            cols = slice(chunk * LANES, (chunk + 1) * LANES)
            padded[chunk, :EDGE] = held[low : low + EDGE, cols] * before
            padded[chunk, EDGE : EDGE + C] = held[low + EDGE : low + EDGE + C, cols]
            padded[chunk, EDGE + C :] = held[low + EDGE + C : low + 2 * EDGE + C, cols] * after
        for chunk in range(width // LANES):
            cols = slice(chunk * LANES, (chunk + 1) * LANES)
            for part in range(0, C, 64):
                total = jnp.zeros((64, LANES), jnp.float32)
                for tap in range(taps_ref.shape[0]):
                    at_row = EDGE - half + part + tap
                    total = total + padded[chunk, at_row : at_row + 64] * taps[tap : tap + 1, cols]
                sum_ref[low + part : low + part + 64, cols] = total


def tail_kernel(
    sum_ref, halo_ref, taps_ref, flags_ref, first_ref, gain_depth_ref, gain_ffn_ref, gain_final_ref,
    w_point_ref, up_own_ref, up_other_ref, down_own_ref, down_other_ref,
    out_ref,
    around, depth, normed, second, hidden, feed,
):
    rows, width = sum_ref.shape
    half = (taps_ref.shape[0] - 1) // 2
    units = up_own_ref.shape[1]
    step = 512
    core = lax.axis_index("mp")
    at = 2 + 3 * core
    same = jnp.where(
        flags_ref[1, pl.ds(at, 1), :] == flags_ref[1, pl.ds(at - 1 + 2 * core, 1), :], 1.0, 0.0
    )
    taps = taps_ref[...].astype(jnp.float32)
    depth[...] = sum_ref[...]
    around[...] = jnp.zeros_like(around)
    for chunk in range(width // LANES):
        cols = slice(chunk * LANES, (chunk + 1) * LANES)
        around[chunk, pl.ds(pl.multiple_of(core * 2 * EDGE, EDGE), EDGE)] = (
            halo_ref[:, cols].astype(jnp.float32) * same
        )
    edge = pl.ds(pl.multiple_of(core * (rows - EDGE), EDGE), EDGE)
    for chunk in range(width // LANES):
        cols = slice(chunk * LANES, (chunk + 1) * LANES)
        total = jnp.zeros((EDGE, LANES), jnp.float32)
        for tap in range(taps_ref.shape[0]):
            at_row = EDGE - half + tap
            total = total + around[chunk, at_row : at_row + EDGE] * taps[tap : tap + 1, cols]
        depth[edge, cols] = depth[edge, cols] + total

    def squash(part):
        value = norm_rows(depth[part], gain_depth_ref[...])
        normed[part] = (value * sigmoid(value)).astype(jnp.bfloat16)

    each(rows, 16, squash)
    second[...] = first_ref[...] + jnp.dot(
        normed[...], w_point_ref[...], preferred_element_type=jnp.float32
    )

    def ffn_norm(part):
        normed[part] = norm_rows(second[part], gain_ffn_ref[...]).astype(jnp.bfloat16)

    each(rows, 16, ffn_norm)
    for group, ref in enumerate((up_own_ref, up_other_ref)):
        for part in range(units // step):
            cols = slice(part * step, (part + 1) * step)
            value = jnp.dot(normed[...], ref[:, cols], preferred_element_type=jnp.float32)
            hidden[group, :, cols] = (value * sigmoid(value)).astype(jnp.bfloat16)
    for part in range(width // 256):
        cols = slice(part * 256, (part + 1) * 256)
        total = 0.0
        for group, ref in enumerate((down_own_ref, down_other_ref)):
            total = total + jnp.dot(
                hidden[group], ref[:, cols], preferred_element_type=jnp.float32
            ).astype(jnp.bfloat16).astype(jnp.float32)
        feed[:, cols] = second[:, cols] + 0.5 * total

    def finish(part):
        out_ref[part] = norm_rows(feed[part], gain_final_ref[...]).astype(jnp.bfloat16)

    each(rows, 16, finish)


def on_device(
    frames,
    gain_attn,
    w_qkv,
    w_out,
    gain_conv,
    w_point_in,
    w_depth,
    gain_depth,
    w_point_out,
    gain_ffn,
    w_up,
    w_down,
    gain_final,
    lengths,
    context,
):
    slab, width = frames.shape
    rows = slab // 2
    local = w_qkv.shape[2]
    window = rows + EDGE
    units = w_up.shape[1]
    tm = lax.axis_size("tm")
    bf16, f32 = jnp.bfloat16, jnp.float32
    shape = jax.ShapeDtypeStruct
    swap = [(0, 1), (1, 0)]

    def row(vec):
        return vec.reshape(1, -1)

    w_planes = jnp.transpose(w_qkv, (1, 0, 2))
    sent, normed = pl.pallas_call(
        send_kernel,
        out_shape=(shape((rows, width), bf16), shape((slab, width), bf16)),
        in_specs=[VMEM] * 2,
        out_specs=(VMEM,) * 2,
        compiler_params=params(8),
        cost_estimate=cost(0, 2 * rows * width * 2),
        name="send_norm",
    )(frames, row(gain_attn))
    up_held, down_held, sent = lax.optimization_barrier((w_up, w_down, sent))
    up_other = lax.ppermute(up_held, "mp", swap)
    down_other = lax.ppermute(down_held, "mp", swap)
    near_mine = lax.ppermute(sent, "tm", [(i, i + 1) for i in range(tm - 1)])
    far_mine = lax.ppermute(sent, "tm", [(i, i + 2) for i in range(tm - 2)])
    qkv, flags = pl.pallas_call(
        own_kernel,
        grid=(3,),
        out_shape=(shape((3, slab, local), bf16), shape((2, 8, LANES), f32)),
        in_specs=[
            pl.BlockSpec((slab, width), lambda i: (0, 0)),
            pl.BlockSpec((1, width, local), lambda i: (i, 0, 0)),
            pl.BlockSpec((1, lengths.shape[0]), lambda i: (0, 0)),
            pl.BlockSpec((1, lengths.shape[0]), lambda i: (0, 0)),
        ],
        out_specs=(
            pl.BlockSpec((1, slab, local), lambda i: (i, 0, 0)),
            pl.BlockSpec((2, 8, LANES), lambda i: (0, 0, 0)),
        ),
        compiler_params=params(16),
        cost_estimate=cost(slab * width * 3 * local, width * 3 * local * 2, EARLY),
        name="own_qkv",
    )(normed, w_planes, row(lengths), row(context))
    partial = (shape((slab, local), f32),) * 3
    own_parts = pl.pallas_call(
        self_kernel,
        out_shape=partial,
        in_specs=[VMEM] * 2,
        out_specs=(VMEM,) * 3,
        compiler_params=params(16),
        cost_estimate=cost(5 * slab * slab * local, 4 * MIB, EARLY),
        name="own_attention",
    )(qkv, flags)
    near_mine, own_parts = lax.optimization_barrier((near_mine, own_parts))
    near_theirs = [lax.ppermute(near_mine[at : at + C], "mp", swap) for at in range(0, rows, C)]
    near_parts = pl.pallas_call(
        near_kernel,
        out_shape=partial,
        in_specs=[VMEM] * 9,
        out_specs=(VMEM,) * 3,
        scratch_shapes=[
            pltpu.VMEM((slab, width), bf16),
            pltpu.VMEM((slab, local), bf16),
            pltpu.VMEM((slab, local), bf16),
        ],
        compiler_params=params(16),
        cost_estimate=cost(slab * width * 2 * local + 8 * slab * slab * local, 8 * MIB, MIDDLE),
        name="near_attention",
    )(qkv, near_mine, *near_theirs, w_planes, flags, *own_parts)
    far_mine, near_parts = lax.optimization_barrier((far_mine, near_parts))
    far_theirs = lax.ppermute(far_mine, "mp", swap)
    heads, to_other = pl.pallas_call(
        far_kernel,
        out_shape=(shape((slab, local), bf16), shape((window, width), bf16)),
        in_specs=[VMEM] * 9,
        out_specs=(VMEM,) * 2,
        scratch_shapes=[
            pltpu.VMEM((slab, width), bf16),
            pltpu.VMEM((slab, local), bf16),
            pltpu.VMEM((slab, local), bf16),
        ],
        compiler_params=params(16),
        cost_estimate=cost(slab * width * 2 * local + 3 * slab * slab * local, 10 * MIB, LATE),
        name="far_attention",
    )(qkv, far_mine, far_theirs, w_planes, flags, *near_parts, w_out)
    from_other = lax.ppermute(to_other, "mp", swap)
    base = pl.pallas_call(
        base_kernel,
        out_shape=shape((window, width), f32),
        in_specs=[VMEM] * 3,
        out_specs=VMEM,
        compiler_params=params(12),
        cost_estimate=cost(window * width * local, 3 * MIB),
        name="out_projection",
    )(heads, w_out, frames)
    gated, edge, first_res = pl.pallas_call(
        gate_kernel,
        out_shape=(
            shape((window, width), bf16),
            shape((EDGE, width), bf16),
            shape((rows, width), f32),
        ),
        in_specs=[VMEM] * 4,
        out_specs=(VMEM,) * 3,
        scratch_shapes=[pltpu.VMEM((window, width), bf16), pltpu.VMEM((window, width), f32)],
        compiler_params=params(16),
        cost_estimate=cost(window * width * 2 * width, 5 * MIB),
        name="gated_units",
    )(base, from_other, row(gain_conv), w_point_in)
    halo_pairs = [(2 * i + 1, 2 * i + 2) for i in range(tm - 1)]
    halo = lax.ppermute(edge, ("tm", "mp"), halo_pairs + [(b, a) for a, b in halo_pairs])
    depth_sum = pl.pallas_call(
        conv_kernel,
        out_shape=shape((rows, width), f32),
        in_specs=[VMEM] * 3,
        out_specs=VMEM,
        scratch_shapes=[
            pltpu.VMEM((rows + 2 * EDGE, width), f32),
            pltpu.VMEM((width // LANES, C + 2 * EDGE, LANES), f32),
        ],
        compiler_params=params(12),
        cost_estimate=cost(rows * width * 512, MIB),
        name="depthwise",
    )(gated, w_depth, flags)
    return pl.pallas_call(
        tail_kernel,
        out_shape=shape((rows, width), bf16),
        in_specs=[VMEM] * 13,
        out_specs=VMEM,
        scratch_shapes=[
            pltpu.VMEM((width // LANES, 3 * EDGE, LANES), f32),
            pltpu.VMEM((rows, width), f32),
            pltpu.VMEM((rows, width), bf16),
            pltpu.VMEM((rows, width), f32),
            pltpu.VMEM((2, rows, units), bf16),
            pltpu.VMEM((rows, width), f32),
        ],
        compiler_params=params(12),
        cost_estimate=cost(rows * width * 9 * width, 18 * MIB),
        name="tail",
    )(
        depth_sum, halo, w_depth, flags, first_res, row(gain_depth), row(gain_ffn),
        row(gain_final), w_point_out, w_up, up_other, w_down, down_other,
    )


def solution(mesh):
    in_specs = (
        P("tm", None),
        P(),
        P(None, None, "mp"),
        P("mp", None),
        P(),
        P(),
        P(),
        P(),
        P(),
        P(),
        P(None, "mp"),
        P("mp", None),
        P(),
        P(),
        P(),
    )
    out_specs = P(("tm", "mp"), None)
    return jax.shard_map(
        on_device, mesh=mesh, in_specs=in_specs, out_specs=out_specs, check_vma=False
    )
```

```python
import jax
import jax.numpy as jnp
from jax import lax
from jax.experimental import pallas as pl
from jax.experimental.pallas import tpu as pltpu
from jax.sharding import PartitionSpec as P

HD = 64
C = 128
LANES = 128
EPSILON = 1e-05
NEGATIVE = -1e30
EDGE = 16
MIB = 1 << 20
EARLY = 0.001
LATE = 13.4
MIDDLE = 0.001
ROOMY = 16
SPARE = 32
VMEM = pl.BlockSpec(memory_space=pltpu.VMEM)
HBM = pl.BlockSpec(memory_space=pltpu.HBM)


def in_hbm(array):
    return pltpu.with_memory_space_constraint(array, pltpu.HBM)


def params(limit):
    return pltpu.CompilerParams(vmem_limit_bytes=limit * MIB)


def cost(macs, read, share=1.0):
    return pl.CostEstimate(
        flops=int(2 * macs * share), bytes_accessed=int(read * share), transcendentals=0
    )


def norm_rows(values, gain):
    centred = values - jnp.mean(values, axis=-1, keepdims=True)
    variance = jnp.mean(centred * centred, axis=-1, keepdims=True)
    return centred * lax.rsqrt(variance + EPSILON) * gain


def sigmoid(values):
    return 0.5 + 0.5 * jnp.tanh(0.5 * values)


def each(rows, step, body):
    for first in range(0, rows, step):
        body(slice(first, first + step))


def begin(pairs, sem):
    copies = [
        pltpu.make_async_copy(source, target, sem.at[number])
        for number, (source, target) in enumerate(pairs)
    ]
    for copy in copies:
        copy.start()
    return copies


def send_kernel(frames_ref, gain_ref, sent_ref, far_ref, normed_ref, frames, gain, sem):
    rows = sent_ref.shape[0]
    parts = [slice(0, rows), slice(rows, 2 * rows)]
    copies = begin(
        [(gain_ref, gain)] + [(frames_ref.at[part], frames.at[part]) for part in parts], sem
    )

    def body(part):
        normed_ref[part] = norm_rows(frames[part].astype(jnp.float32), gain[...]).astype(
            jnp.bfloat16
        )

    copies[0].wait()
    for copy, whole in zip(copies[1:], parts):
        copy.wait()
        for first in range(whole.start, whole.stop, 16):
            body(slice(first, first + 16))
    first = pl.multiple_of(lax.axis_index("mp") * rows, rows)
    half = normed_ref[pl.ds(first, rows)]
    sent_ref[...] = half
    far_ref[:rows] = half
    far_ref[rows:] = half[: far_ref.shape[0] - rows]


def own_kernel(
    normed_ref, w_ref, lengths_ref, context_ref, qkv_ref, flags_ref, w, lengths, context, sem
):
    rows = normed_ref.shape[0]
    copies = begin(
        [(lengths_ref, lengths), (context_ref, context)]
        + [(w_ref.at[plane], w.at[plane]) for plane in range(3)],
        sem,
    )
    copies[0].wait()
    copies[1].wait()
    count = lengths.shape[1]
    sizes = jnp.broadcast_to(lengths[...], (8, count)).astype(jnp.float32)
    before = (
        lax.broadcasted_iota(jnp.int32, (count, count), 0)
        < lax.broadcasted_iota(jnp.int32, (count, count), 1)
    ).astype(jnp.float32).astype(jnp.bfloat16)
    start = jnp.dot(sizes.astype(jnp.bfloat16), before, preferred_element_type=jnp.float32)
    stretch = (
        lax.axis_index("tm") * (rows // C) - 2 + lax.broadcasted_iota(jnp.int32, (8, count), 0)
    ).astype(jnp.float32)
    member = jnp.where((start <= stretch) & (stretch < start + sizes), 1.0, 0.0)
    allowed = jnp.broadcast_to(context[...], (8, count)).astype(jnp.float32)
    number = lax.broadcasted_iota(jnp.int32, (8, count), 1).astype(jnp.float32) + 1.0
    opening = jnp.sum(member * start, axis=1, keepdims=True)
    reached = jnp.sum(member * allowed, axis=1, keepdims=True)
    label = jnp.sum(member * number, axis=1, keepdims=True)
    flags_ref[0] = jnp.maximum(stretch[:, :LANES] - reached, opening)
    flags_ref[1] = jnp.broadcast_to(label, (8, LANES))
    for plane in range(3):
        copies[2 + plane].wait()
        product = jnp.dot(normed_ref[...], w[plane], preferred_element_type=jnp.float32)
        if plane == 0:
            product = product * HD**-0.5
        qkv_ref[plane] = product.astype(jnp.bfloat16)


def bias_row(lowest, stretches):
    return jnp.concatenate(
        [jnp.where(stretch >= lowest, 0.0, NEGATIVE) for stretch in stretches], axis=1
    )


def attend_all(queries, keys, values, biases):
    first_head = lax.broadcasted_iota(jnp.int32, (C, LANES), 1) < HD
    zero = jnp.zeros_like(queries[0])
    stacked = []
    for query in queries:
        stacked += [jnp.where(first_head, query, zero), jnp.where(first_head, zero, query)]
    scores = lax.dot_general(
        jnp.concatenate(stacked, axis=0),
        keys,
        (((1,), (1,)), ((), ())),
        preferred_element_type=jnp.float32,
    )
    raised, tops = [], []
    for i, bias in enumerate(biases):
        part = scores[2 * i * C : 2 * (i + 1) * C] + bias
        highest = jnp.max(part, axis=1, keepdims=True)
        raised.append(jnp.exp(part - highest).astype(jnp.bfloat16))
        tops.append(highest)
    wide = jnp.concatenate([values, jnp.ones_like(values)], axis=1)
    mixed = jnp.dot(jnp.concatenate(raised, axis=0), wide, preferred_element_type=jnp.float32)
    found = []
    for i, highest in enumerate(tops):
        one = mixed[2 * i * C : (2 * i + 1) * C]
        two = mixed[(2 * i + 1) * C : 2 * (i + 1) * C]
        total = jnp.where(first_head, one[:, :LANES], two[:, :LANES])
        weight = jnp.where(first_head, one[:, LANES:], two[:, LANES:])
        top = jnp.where(
            first_head,
            jnp.broadcast_to(highest[:C], (C, LANES)),
            jnp.broadcast_to(highest[C:], (C, LANES)),
        )
        found.append((total, top, weight))
    return found


def attend(query, keys, values, bias):
    return attend_all([query], keys, values, [bias])[0]


def place(normed, mine_ref, theirs_ref):
    rows = normed.shape[0] // 2
    core = lax.axis_index("mp")
    normed[pl.ds(pl.multiple_of(core * rows, rows), rows)] = mine_ref[:rows]
    normed[pl.ds(pl.multiple_of((1 - core) * rows, rows), rows)] = theirs_ref[:rows]


def merged(parts, total, top, weight):
    other_total, other_top, other_weight = parts
    highest = jnp.maximum(other_top, top)
    other_part = jnp.exp(other_top - highest)
    part = jnp.exp(top - highest)
    return (
        other_total * other_part + total * part,
        highest,
        other_weight * other_part + weight * part,
    )


def self_kernel(qkv_ref, flags_ref, total_ref, top_ref, weight_ref):
    slab, width = qkv_ref.shape[1:]
    count = slab // C
    first = lax.axis_index("tm") * count
    for i in range(count):
        rows = slice(i * C, (i + 1) * C)
        lowest = flags_ref[0, 2 + i : 3 + i, :]
        bias = bias_row(lowest, [(first + n).astype(jnp.float32) for n in range(i + 1)])
        for pair in range(width // LANES):
            cols = slice(pair * LANES, (pair + 1) * LANES)
            seen = slice(0, (i + 1) * C)
            total_ref[rows, cols], top_ref[rows, cols], weight_ref[rows, cols] = attend(
                qkv_ref[0, rows, cols], qkv_ref[1, seen, cols], qkv_ref[2, seen, cols], bias
            )


def near_kernel(
    qkv_ref, mine_ref, theirs_ref, w_ref, flags_ref,
    own_total_ref, own_top_ref, own_weight_ref,
    total_ref, top_ref, weight_ref,
    normed, keys, values,
):
    slab, width = qkv_ref.shape[1:]
    count = slab // C
    place(normed, mine_ref, theirs_ref)
    keys[...] = jnp.dot(normed[...], w_ref[1], preferred_element_type=jnp.float32).astype(
        jnp.bfloat16
    )
    values[...] = jnp.dot(normed[...], w_ref[2], preferred_element_type=jnp.float32).astype(
        jnp.bfloat16
    )
    first = lax.axis_index("tm") * count - count
    every = [slice(i * C, (i + 1) * C) for i in range(count)]
    seen = [(first + n).astype(jnp.float32) for n in range(count)]
    biases = [bias_row(flags_ref[0, 2 + i : 3 + i, :], seen) for i in range(count)]
    for pair in range(width // LANES):
        cols = slice(pair * LANES, (pair + 1) * LANES)
        found = attend_all(
            [qkv_ref[0, rows, cols] for rows in every], keys[:, cols], values[:, cols], biases
        )
        for rows, part in zip(every, found):
            parts = own_total_ref[rows, cols], own_top_ref[rows, cols], own_weight_ref[rows, cols]
            total_ref[rows, cols], top_ref[rows, cols], weight_ref[rows, cols] = merged(
                parts, *part
            )


def far_kernel(
    qkv_ref, mine_ref, theirs_ref, w_ref, flags_ref, total_ref, top_ref, weight_ref, w_out_ref,
    heads_ref, sent_ref, normed, keys, values,
):
    slab, width = qkv_ref.shape[1:]
    count = slab // C
    place(normed, mine_ref, theirs_ref)
    keys[...] = jnp.dot(normed[...], w_ref[1], preferred_element_type=jnp.float32).astype(
        jnp.bfloat16
    )
    values[...] = jnp.dot(normed[...], w_ref[2], preferred_element_type=jnp.float32).astype(
        jnp.bfloat16
    )
    first = lax.axis_index("tm") * count - 2 * count
    for i in range(count):
        rows = slice(i * C, (i + 1) * C)
        lowest = flags_ref[0, 2 + i : 3 + i, :]
        bias = bias_row(lowest, [(first + n).astype(jnp.float32) for n in range(i, count)])
        for pair in range(width // LANES):
            cols = slice(pair * LANES, (pair + 1) * LANES)
            total, top, weight = attend(
                qkv_ref[0, rows, cols], keys[i * C :, cols], values[i * C :, cols], bias
            )
            parts = total_ref[rows, cols], top_ref[rows, cols], weight_ref[rows, cols]
            total, _, weight = merged(parts, total, top, weight)
            heads_ref[rows, cols] = (total / weight).astype(jnp.bfloat16)
    window = sent_ref.shape[0]
    other = (1 - lax.axis_index("mp")) * (slab - window)
    sent_ref[...] = jnp.dot(
        heads_ref[pl.ds(pl.multiple_of(other, EDGE), window)],
        w_out_ref[...],
        preferred_element_type=jnp.float32,
    ).astype(jnp.bfloat16)


def base_kernel(heads_ref, w_out_ref, frames_ref, base_ref):
    slab = heads_ref.shape[0]
    window = base_ref.shape[0]
    first = pl.multiple_of(lax.axis_index("mp") * (slab - window), EDGE)
    base_ref[...] = frames_ref[pl.ds(first, window)].astype(jnp.float32) + jnp.dot(
        heads_ref[pl.ds(first, window)], w_out_ref[...], preferred_element_type=jnp.float32
    ).astype(jnp.bfloat16).astype(jnp.float32)


def gate_kernel(
    base_ref, got_ref, gain_ref, w_ref, gated_ref, edge_ref, first_ref, normed, held
):
    window, width = base_ref.shape
    rows = first_ref.shape[0]

    def body(part):
        value = base_ref[part] + got_ref[part].astype(jnp.float32)
        held[part] = value
        normed[part] = norm_rows(value, gain_ref[...]).astype(jnp.bfloat16)

    each(window, 16, body)
    for part in range(0, width, 256):
        cols = slice(part, part + 256)
        value = jnp.dot(normed[...], w_ref[:, cols], preferred_element_type=jnp.float32)
        gate = jnp.dot(
            normed[...],
            w_ref[:, width + part : width + part + 256],
            preferred_element_type=jnp.float32,
        )
        gated_ref[:, cols] = (value * sigmoid(gate)).astype(jnp.bfloat16)
    core = lax.axis_index("mp")
    edge_ref[...] = gated_ref[pl.ds(pl.multiple_of(core * (window - EDGE), EDGE), EDGE)]
    first_ref[...] = held[pl.ds(pl.multiple_of(core * (window - rows), EDGE), rows)]


def conv_kernel(gated_ref, taps_ref, flags_ref, sum_ref, held, padded):
    window, width = gated_ref.shape
    rows = sum_ref.shape[0]
    half = (taps_ref.shape[0] - 1) // 2
    core = lax.axis_index("mp")
    zeros = jnp.zeros((EDGE, width), jnp.float32)
    held[:EDGE] = zeros
    held[rows + EDGE :] = zeros
    held[pl.ds(pl.multiple_of((1 - core) * EDGE, EDGE), window)] = gated_ref[...].astype(
        jnp.float32
    )
    taps = taps_ref[...].astype(jnp.float32)
    for stretch in range(rows // C):
        at = 2 + (rows // C) * core + stretch
        label = flags_ref[1, pl.ds(at, 1), :]
        before = jnp.where(flags_ref[1, pl.ds(at - 1, 1), :] == label, 1.0, 0.0)
        after = jnp.where(flags_ref[1, pl.ds(at + 1, 1), :] == label, 1.0, 0.0)
        low = stretch * C
        for chunk in range(width // LANES):
            cols = slice(chunk * LANES, (chunk + 1) * LANES)
            padded[chunk, :EDGE] = held[low : low + EDGE, cols] * before
            padded[chunk, EDGE : EDGE + C] = held[low + EDGE : low + EDGE + C, cols]
            padded[chunk, EDGE + C :] = held[low + EDGE + C : low + 2 * EDGE + C, cols] * after
        for chunk in range(width // LANES):
            cols = slice(chunk * LANES, (chunk + 1) * LANES)
            for part in range(0, C, 64):
                total = jnp.zeros((64, LANES), jnp.float32)
                for tap in range(taps_ref.shape[0]):
                    at_row = EDGE - half + part + tap
                    total = total + padded[chunk, at_row : at_row + 64] * taps[tap : tap + 1, cols]
                sum_ref[low + part : low + part + 64, cols] = total


def tail_kernel(
    sum_ref, halo_ref, taps_ref, flags_ref, first_ref, gain_depth_ref, gain_ffn_ref, gain_final_ref,
    w_point_ref, up_own_ref, up_other_ref, down_own_ref, down_other_ref,
    out_ref,
    around, depth, normed, second, hidden, feed,
):
    rows, width = sum_ref.shape
    half = (taps_ref.shape[0] - 1) // 2
    units = up_own_ref.shape[1]
    step = 512
    core = lax.axis_index("mp")
    at = 2 + 3 * core
    same = jnp.where(
        flags_ref[1, pl.ds(at, 1), :] == flags_ref[1, pl.ds(at - 1 + 2 * core, 1), :], 1.0, 0.0
    )
    taps = taps_ref[...].astype(jnp.float32)
    depth[...] = sum_ref[...]
    around[...] = jnp.zeros_like(around)
    for chunk in range(width // LANES):
        cols = slice(chunk * LANES, (chunk + 1) * LANES)
        around[chunk, pl.ds(pl.multiple_of(core * 2 * EDGE, EDGE), EDGE)] = (
            halo_ref[:, cols].astype(jnp.float32) * same
        )
    edge = pl.ds(pl.multiple_of(core * (rows - EDGE), EDGE), EDGE)
    for chunk in range(width // LANES):
        cols = slice(chunk * LANES, (chunk + 1) * LANES)
        total = jnp.zeros((EDGE, LANES), jnp.float32)
        for tap in range(taps_ref.shape[0]):
            at_row = EDGE - half + tap
            total = total + around[chunk, at_row : at_row + EDGE] * taps[tap : tap + 1, cols]
        depth[edge, cols] = depth[edge, cols] + total

    def squash(part):
        value = norm_rows(depth[part], gain_depth_ref[...])
        normed[part] = (value * sigmoid(value)).astype(jnp.bfloat16)

    each(rows, 16, squash)
    second[...] = first_ref[...] + jnp.dot(
        normed[...], w_point_ref[...], preferred_element_type=jnp.float32
    )

    def ffn_norm(part):
        normed[part] = norm_rows(second[part], gain_ffn_ref[...]).astype(jnp.bfloat16)

    each(rows, 16, ffn_norm)
    for group, ref in enumerate((up_own_ref, up_other_ref)):
        for part in range(units // step):
            cols = slice(part * step, (part + 1) * step)
            value = jnp.dot(normed[...], ref[:, cols], preferred_element_type=jnp.float32)
            hidden[group, :, cols] = (value * sigmoid(value)).astype(jnp.bfloat16)
    for part in range(width // 256):
        cols = slice(part * 256, (part + 1) * 256)
        total = 0.0
        for group, ref in enumerate((down_own_ref, down_other_ref)):
            total = total + jnp.dot(
                hidden[group], ref[:, cols], preferred_element_type=jnp.float32
            ).astype(jnp.bfloat16).astype(jnp.float32)
        feed[:, cols] = second[:, cols] + 0.5 * total

    def finish(part):
        out_ref[part] = norm_rows(feed[part], gain_final_ref[...]).astype(jnp.bfloat16)

    each(rows, 16, finish)


def on_device(
    frames,
    gain_attn,
    w_qkv,
    w_out,
    gain_conv,
    w_point_in,
    w_depth,
    gain_depth,
    w_point_out,
    gain_ffn,
    w_up,
    w_down,
    gain_final,
    lengths,
    context,
):
    slab, width = frames.shape
    rows = slab // 2
    local = w_qkv.shape[2]
    window = rows + EDGE
    units = w_up.shape[1]
    tm = lax.axis_size("tm")
    bf16, f32 = jnp.bfloat16, jnp.float32
    shape = jax.ShapeDtypeStruct
    swap = [(0, 1), (1, 0)]

    def row(vec):
        return vec.reshape(1, -1)

    w_planes = jnp.transpose(w_qkv, (1, 0, 2))
    sent, sent_far, normed = pl.pallas_call(
        send_kernel,
        out_shape=(
            shape((rows, width), bf16),
            shape((rows + SPARE, width), bf16),
            shape((slab, width), bf16),
        ),
        in_specs=[HBM] * 2,
        out_specs=(VMEM,) * 3,
        scratch_shapes=[
            pltpu.VMEM((slab, width), bf16),
            pltpu.VMEM((1, width), f32),
            pltpu.SemaphoreType.DMA((3,)),
        ],
        compiler_params=params(8),
        cost_estimate=cost(0, 2 * rows * width * 2),
        name="send_norm",
    )(in_hbm(frames), in_hbm(row(gain_attn)))
    up_held, down_held, sent = lax.optimization_barrier((w_up, w_down, sent))
    up_other = lax.ppermute(up_held, "mp", swap)
    down_other = lax.ppermute(down_held, "mp", swap)
    near_mine = lax.ppermute(sent, "tm", [(i, i + 1) for i in range(tm - 1)])
    far_mine = lax.ppermute(sent_far, "tm", [(i, i + 2) for i in range(tm - 2)])
    qkv, flags = pl.pallas_call(
        own_kernel,
        out_shape=(shape((3, slab, local), bf16), shape((2, 8, LANES), f32)),
        in_specs=[VMEM] + [HBM] * 3,
        out_specs=(VMEM,) * 2,
        scratch_shapes=[
            pltpu.VMEM((3, width, local), bf16),
            pltpu.VMEM((1, lengths.shape[0]), jnp.int32),
            pltpu.VMEM((1, lengths.shape[0]), jnp.int32),
            pltpu.SemaphoreType.DMA((5,)),
        ],
        compiler_params=params(ROOMY),
        cost_estimate=cost(slab * width * 3 * local, width * 3 * local * 2, EARLY),
        name="own_qkv",
    )(normed, in_hbm(w_planes), in_hbm(row(lengths)), in_hbm(row(context)))
    partial = (shape((slab, local), f32),) * 3
    own_parts = pl.pallas_call(
        self_kernel,
        out_shape=partial,
        in_specs=[VMEM] * 2,
        out_specs=(VMEM,) * 3,
        compiler_params=params(16),
        cost_estimate=cost(5 * slab * slab * local, 4 * MIB, EARLY),
        name="own_attention",
    )(qkv, flags)
    near_mine, own_parts = lax.optimization_barrier((near_mine, own_parts))
    near_theirs = lax.ppermute(near_mine, "mp", swap)
    near_parts = pl.pallas_call(
        near_kernel,
        out_shape=partial,
        in_specs=[VMEM] * 8,
        out_specs=(VMEM,) * 3,
        scratch_shapes=[
            pltpu.VMEM((slab, width), bf16),
            pltpu.VMEM((slab, local), bf16),
            pltpu.VMEM((slab, local), bf16),
        ],
        compiler_params=params(16),
        cost_estimate=cost(slab * width * 2 * local + 8 * slab * slab * local, 8 * MIB, MIDDLE),
        name="near_attention",
    )(qkv, near_mine, near_theirs, w_planes, flags, *own_parts)
    far_mine, near_parts = lax.optimization_barrier((far_mine, near_parts))
    far_theirs = lax.ppermute(far_mine, "mp", swap)
    heads, to_other = pl.pallas_call(
        far_kernel,
        out_shape=(shape((slab, local), bf16), shape((window, width), bf16)),
        in_specs=[VMEM] * 9,
        out_specs=(VMEM,) * 2,
        scratch_shapes=[
            pltpu.VMEM((slab, width), bf16),
            pltpu.VMEM((slab, local), bf16),
            pltpu.VMEM((slab, local), bf16),
        ],
        compiler_params=params(16),
        cost_estimate=cost(slab * width * 2 * local + 3 * slab * slab * local, 10 * MIB, LATE),
        name="far_attention",
    )(qkv, far_mine, far_theirs, w_planes, flags, *near_parts, w_out)
    from_other = lax.ppermute(to_other, "mp", swap)
    base = pl.pallas_call(
        base_kernel,
        out_shape=shape((window, width), f32),
        in_specs=[VMEM] * 3,
        out_specs=VMEM,
        compiler_params=params(12),
        cost_estimate=cost(window * width * local, 3 * MIB),
        name="out_projection",
    )(heads, w_out, frames)
    gated, edge, first_res = pl.pallas_call(
        gate_kernel,
        out_shape=(
            shape((window, width), bf16),
            shape((EDGE, width), bf16),
            shape((rows, width), f32),
        ),
        in_specs=[VMEM] * 4,
        out_specs=(VMEM,) * 3,
        scratch_shapes=[pltpu.VMEM((window, width), bf16), pltpu.VMEM((window, width), f32)],
        compiler_params=params(16),
        cost_estimate=cost(window * width * 2 * width, 5 * MIB),
        name="gated_units",
    )(base, from_other, row(gain_conv), w_point_in)
    halo_pairs = [(2 * i + 1, 2 * i + 2) for i in range(tm - 1)]
    halo = lax.ppermute(edge, ("tm", "mp"), halo_pairs + [(b, a) for a, b in halo_pairs])
    depth_sum = pl.pallas_call(
        conv_kernel,
        out_shape=shape((rows, width), f32),
        in_specs=[VMEM] * 3,
        out_specs=VMEM,
        scratch_shapes=[
            pltpu.VMEM((rows + 2 * EDGE, width), f32),
            pltpu.VMEM((width // LANES, C + 2 * EDGE, LANES), f32),
        ],
        compiler_params=params(12),
        cost_estimate=cost(rows * width * 512, MIB),
        name="depthwise",
    )(gated, w_depth, flags)
    return pl.pallas_call(
        tail_kernel,
        out_shape=shape((rows, width), bf16),
        in_specs=[VMEM] * 13,
        out_specs=VMEM,
        scratch_shapes=[
            pltpu.VMEM((width // LANES, 3 * EDGE, LANES), f32),
            pltpu.VMEM((rows, width), f32),
            pltpu.VMEM((rows, width), bf16),
            pltpu.VMEM((rows, width), f32),
            pltpu.VMEM((2, rows, units), bf16),
            pltpu.VMEM((rows, width), f32),
        ],
        compiler_params=params(12),
        cost_estimate=cost(rows * width * 9 * width, 18 * MIB),
        name="tail",
    )(
        depth_sum, halo, w_depth, flags, first_res, row(gain_depth), row(gain_ffn),
        row(gain_final), w_point_out, w_up, up_other, w_down, down_other,
    )


def solution(mesh):
    in_specs = (
        P("tm", None),
        P(),
        P(None, None, "mp"),
        P("mp", None),
        P(),
        P(),
        P(),
        P(),
        P(),
        P(),
        P(None, "mp"),
        P("mp", None),
        P(),
        P(),
        P(),
    )
    out_specs = P(("tm", "mp"), None)
    return jax.shard_map(
        on_device, mesh=mesh, in_specs=in_specs, out_specs=out_specs, check_vma=False
    )
```

```python
import functools

import jax
import jax.numpy as jnp
from jax import lax
from jax.experimental import pallas as pl
from jax.experimental.pallas import tpu as pltpu
from jax.sharding import PartitionSpec as P

HD = 64
C = 128
LANES = 128
EPSILON = 1e-05
NEGATIVE = -1e30
EDGE = 16
MIB = 1 << 20
EARLY = 0.001
LATE = 13.4
MIDDLE = 0.001
ROOMY = 16
SPARE = 32
VMEM = pl.BlockSpec(memory_space=pltpu.VMEM)
HBM = pl.BlockSpec(memory_space=pltpu.HBM)


def in_hbm(array):
    return pltpu.with_memory_space_constraint(array, pltpu.HBM)


def params(limit):
    return pltpu.CompilerParams(vmem_limit_bytes=limit * MIB)


def cost(macs, read, share=1.0):
    return pl.CostEstimate(
        flops=int(2 * macs * share), bytes_accessed=int(read * share), transcendentals=0
    )


def norm_rows(values, gain):
    centred = values - jnp.mean(values, axis=-1, keepdims=True)
    variance = jnp.mean(centred * centred, axis=-1, keepdims=True)
    return centred * lax.rsqrt(variance + EPSILON) * gain


def sigmoid(values):
    return 0.5 + 0.5 * jnp.tanh(0.5 * values)


def each(rows, step, body):
    for first in range(0, rows, step):
        body(slice(first, first + step))


def begin(pairs, sem):
    copies = [
        pltpu.make_async_copy(source, target, sem.at[number])
        for number, (source, target) in enumerate(pairs)
    ]
    for copy in copies:
        copy.start()
    return copies


def send_kernel(frames_ref, gain_ref, sent_ref, far_ref, normed_ref, frames, gain, sem):
    rows = sent_ref.shape[0]
    parts = [slice(0, rows), slice(rows, 2 * rows)]
    copies = begin(
        [(gain_ref, gain)] + [(frames_ref.at[part], frames.at[part]) for part in parts], sem
    )

    def body(part):
        normed_ref[part] = norm_rows(frames[part].astype(jnp.float32), gain[...]).astype(
            jnp.bfloat16
        )

    copies[0].wait()
    for copy, whole in zip(copies[1:], parts):
        copy.wait()
        for first in range(whole.start, whole.stop, 16):
            body(slice(first, first + 16))
    first = pl.multiple_of(lax.axis_index("mp") * rows, rows)
    half = normed_ref[pl.ds(first, rows)]
    sent_ref[...] = half
    far_ref[:rows] = half
    far_ref[rows:] = half[: far_ref.shape[0] - rows]


def own_kernel(
    normed_ref, w_ref, lengths_ref, context_ref, qkv_ref, flags_ref, w, lengths, context, sem
):
    rows = normed_ref.shape[0]
    copies = begin(
        [(lengths_ref, lengths), (context_ref, context)]
        + [(w_ref.at[plane], w.at[plane]) for plane in range(3)],
        sem,
    )
    copies[0].wait()
    copies[1].wait()
    count = lengths.shape[1]
    sizes = jnp.broadcast_to(lengths[...], (8, count)).astype(jnp.float32)
    before = (
        lax.broadcasted_iota(jnp.int32, (count, count), 0)
        < lax.broadcasted_iota(jnp.int32, (count, count), 1)
    ).astype(jnp.float32).astype(jnp.bfloat16)
    start = jnp.dot(sizes.astype(jnp.bfloat16), before, preferred_element_type=jnp.float32)
    stretch = (
        lax.axis_index("tm") * (rows // C) - 2 + lax.broadcasted_iota(jnp.int32, (8, count), 0)
    ).astype(jnp.float32)
    member = jnp.where((start <= stretch) & (stretch < start + sizes), 1.0, 0.0)
    allowed = jnp.broadcast_to(context[...], (8, count)).astype(jnp.float32)
    number = lax.broadcasted_iota(jnp.int32, (8, count), 1).astype(jnp.float32) + 1.0
    opening = jnp.sum(member * start, axis=1, keepdims=True)
    reached = jnp.sum(member * allowed, axis=1, keepdims=True)
    label = jnp.sum(member * number, axis=1, keepdims=True)
    flags_ref[0] = jnp.maximum(stretch[:, :LANES] - reached, opening)
    flags_ref[1] = jnp.broadcast_to(label, (8, LANES))
    for plane in range(3):
        copies[2 + plane].wait()
        product = jnp.dot(normed_ref[...], w[plane], preferred_element_type=jnp.float32)
        if plane == 0:
            product = product * HD**-0.5
        qkv_ref[plane] = product.astype(jnp.bfloat16)


def bias_row(lowest, stretches):
    return jnp.concatenate(
        [jnp.where(stretch >= lowest, 0.0, NEGATIVE) for stretch in stretches], axis=1
    )


def attend_all(queries, keys, values, biases):
    first_head = lax.broadcasted_iota(jnp.int32, (C, LANES), 1) < HD
    zero = jnp.zeros_like(queries[0])
    stacked = []
    for query in queries:
        stacked += [jnp.where(first_head, query, zero), jnp.where(first_head, zero, query)]
    scores = lax.dot_general(
        jnp.concatenate(stacked, axis=0),
        keys,
        (((1,), (1,)), ((), ())),
        preferred_element_type=jnp.float32,
    )
    raised, tops = [], []
    for i, bias in enumerate(biases):
        part = scores[2 * i * C : 2 * (i + 1) * C] + bias
        highest = jnp.max(part, axis=1, keepdims=True)
        raised.append(jnp.exp(part - highest).astype(jnp.bfloat16))
        tops.append(highest)
    wide = jnp.concatenate([values, jnp.ones_like(values)], axis=1)
    mixed = jnp.dot(jnp.concatenate(raised, axis=0), wide, preferred_element_type=jnp.float32)
    found = []
    for i, highest in enumerate(tops):
        one = mixed[2 * i * C : (2 * i + 1) * C]
        two = mixed[(2 * i + 1) * C : 2 * (i + 1) * C]
        total = jnp.where(first_head, one[:, :LANES], two[:, :LANES])
        weight = jnp.where(first_head, one[:, LANES:], two[:, LANES:])
        top = jnp.where(
            first_head,
            jnp.broadcast_to(highest[:C], (C, LANES)),
            jnp.broadcast_to(highest[C:], (C, LANES)),
        )
        found.append((total, top, weight))
    return found


def attend(query, keys, values, bias):
    return attend_all([query], keys, values, [bias])[0]


def merged(parts, total, top, weight):
    other_total, other_top, other_weight = parts
    highest = jnp.maximum(other_top, top)
    other_part = jnp.exp(other_top - highest)
    part = jnp.exp(top - highest)
    return (
        other_total * other_part + total * part,
        highest,
        other_weight * other_part + weight * part,
    )


def self_kernel(qkv_ref, flags_ref, total_ref, top_ref, weight_ref):
    slab, width = qkv_ref.shape[1:]
    count = slab // C
    first = lax.axis_index("tm") * count
    for i in range(count):
        rows = slice(i * C, (i + 1) * C)
        lowest = flags_ref[0, 2 + i : 3 + i, :]
        bias = bias_row(lowest, [(first + n).astype(jnp.float32) for n in range(i + 1)])
        for pair in range(width // LANES):
            cols = slice(pair * LANES, (pair + 1) * LANES)
            seen = slice(0, (i + 1) * C)
            total_ref[rows, cols], top_ref[rows, cols], weight_ref[rows, cols] = attend(
                qkv_ref[0, rows, cols], qkv_ref[1, seen, cols], qkv_ref[2, seen, cols], bias
            )


def near_kernel(
    theirs, qkv_ref, rows_ref, w_ref, flags_ref, own_total_ref, own_top_ref, own_weight_ref,
    total_ref, top_ref, weight_ref,
    keys, values,
):
    slab, width = qkv_ref.shape[1:]
    count = slab // C
    here = rows_ref.shape[0] // C
    keys[...] = jnp.dot(rows_ref[...], w_ref[1], preferred_element_type=jnp.float32).astype(
        jnp.bfloat16
    )
    values[...] = jnp.dot(rows_ref[...], w_ref[2], preferred_element_type=jnp.float32).astype(
        jnp.bfloat16
    )
    core = lax.axis_index("mp")
    half = 1 - core if theirs else core
    first = lax.axis_index("tm") * count - count + half * here
    every = [slice(i * C, (i + 1) * C) for i in range(count)]
    seen = [(first + n).astype(jnp.float32) for n in range(here)]
    biases = [bias_row(flags_ref[0, 2 + i : 3 + i, :], seen) for i in range(count)]
    for pair in range(width // LANES):
        cols = slice(pair * LANES, (pair + 1) * LANES)
        found = attend_all(
            [qkv_ref[0, rows, cols] for rows in every], keys[:, cols], values[:, cols], biases
        )
        for rows, part in zip(every, found):
            parts = own_total_ref[rows, cols], own_top_ref[rows, cols], own_weight_ref[rows, cols]
            total_ref[rows, cols], top_ref[rows, cols], weight_ref[rows, cols] = merged(
                parts, *part
            )


def far_half(theirs, qkv_ref, rows_ref, w_ref, flags_ref, parts_refs, keys, values, put):
    slab, width = qkv_ref.shape[1:]
    count = slab // C
    here = keys.shape[0] // C
    keys[...] = jnp.dot(
        rows_ref[: here * C], w_ref[1], preferred_element_type=jnp.float32
    ).astype(jnp.bfloat16)
    values[...] = jnp.dot(
        rows_ref[: here * C], w_ref[2], preferred_element_type=jnp.float32
    ).astype(jnp.bfloat16)
    core = lax.axis_index("mp")
    half = 1 - core if theirs else core
    first = lax.axis_index("tm") * count - 2 * count

    def work(side):
        for i in range(count):
            rows = slice(i * C, (i + 1) * C)
            skip = max(0, i - side * here)
            seen = slice(skip * C, here * C)
            lowest = flags_ref[0, 2 + i : 3 + i, :]
            stretches = range(side * here + skip, (side + 1) * here)
            for pair in range(width // LANES):
                cols = slice(pair * LANES, (pair + 1) * LANES)
                parts = tuple(ref[rows, cols] for ref in parts_refs)
                if stretches:
                    bias = bias_row(lowest, [(first + n).astype(jnp.float32) for n in stretches])
                    found = attend(qkv_ref[0, rows, cols], keys[seen, cols], values[seen, cols], bias)
                    parts = merged(parts, *found)
                put(rows, cols, parts)

    for side in range(2):
        pl.when(half == side)(functools.partial(work, side))


def far_mine_kernel(
    qkv_ref, rows_ref, w_ref, flags_ref, near_total_ref, near_top_ref, near_weight_ref,
    total_ref, top_ref, weight_ref,
    keys, values,
):
    def put(rows, cols, parts):
        total_ref[rows, cols], top_ref[rows, cols], weight_ref[rows, cols] = parts

    near_refs = near_total_ref, near_top_ref, near_weight_ref
    far_half(False, qkv_ref, rows_ref, w_ref, flags_ref, near_refs, keys, values, put)


def far_theirs_kernel(
    qkv_ref, rows_ref, w_ref, flags_ref, total_ref, top_ref, weight_ref, w_out_ref,
    heads_ref, sent_ref,
    keys, values,
):
    slab = qkv_ref.shape[1]

    def put(rows, cols, parts):
        total, _, weight = parts
        heads_ref[rows, cols] = (total / weight).astype(jnp.bfloat16)

    parts_refs = total_ref, top_ref, weight_ref
    far_half(True, qkv_ref, rows_ref, w_ref, flags_ref, parts_refs, keys, values, put)
    window = sent_ref.shape[0]
    other = (1 - lax.axis_index("mp")) * (slab - window)
    sent_ref[...] = jnp.dot(
        heads_ref[pl.ds(pl.multiple_of(other, EDGE), window)],
        w_out_ref[...],
        preferred_element_type=jnp.float32,
    ).astype(jnp.bfloat16)


def base_kernel(heads_ref, w_out_ref, frames_ref, base_ref):
    slab = heads_ref.shape[0]
    window = base_ref.shape[0]
    first = pl.multiple_of(lax.axis_index("mp") * (slab - window), EDGE)
    base_ref[...] = frames_ref[pl.ds(first, window)].astype(jnp.float32) + jnp.dot(
        heads_ref[pl.ds(first, window)], w_out_ref[...], preferred_element_type=jnp.float32
    ).astype(jnp.bfloat16).astype(jnp.float32)


def gate_kernel(
    base_ref, got_ref, gain_ref, w_ref, gated_ref, edge_ref, first_ref, normed, held
):
    window, width = base_ref.shape
    rows = first_ref.shape[0]

    def body(part):
        value = base_ref[part] + got_ref[part].astype(jnp.float32)
        held[part] = value
        normed[part] = norm_rows(value, gain_ref[...]).astype(jnp.bfloat16)

    each(window, 16, body)
    for part in range(0, width, 256):
        cols = slice(part, part + 256)
        value = jnp.dot(normed[...], w_ref[:, cols], preferred_element_type=jnp.float32)
        gate = jnp.dot(
            normed[...],
            w_ref[:, width + part : width + part + 256],
            preferred_element_type=jnp.float32,
        )
        gated_ref[:, cols] = (value * sigmoid(gate)).astype(jnp.bfloat16)
    core = lax.axis_index("mp")
    edge_ref[...] = gated_ref[pl.ds(pl.multiple_of(core * (window - EDGE), EDGE), EDGE)]
    first_ref[...] = held[pl.ds(pl.multiple_of(core * (window - rows), EDGE), rows)]


def conv_kernel(gated_ref, taps_ref, flags_ref, sum_ref, held, padded):
    window, width = gated_ref.shape
    rows = sum_ref.shape[0]
    half = (taps_ref.shape[0] - 1) // 2
    core = lax.axis_index("mp")
    zeros = jnp.zeros((EDGE, width), jnp.float32)
    held[:EDGE] = zeros
    held[rows + EDGE :] = zeros
    held[pl.ds(pl.multiple_of((1 - core) * EDGE, EDGE), window)] = gated_ref[...].astype(
        jnp.float32
    )
    taps = taps_ref[...].astype(jnp.float32)
    for stretch in range(rows // C):
        at = 2 + (rows // C) * core + stretch
        label = flags_ref[1, pl.ds(at, 1), :]
        before = jnp.where(flags_ref[1, pl.ds(at - 1, 1), :] == label, 1.0, 0.0)
        after = jnp.where(flags_ref[1, pl.ds(at + 1, 1), :] == label, 1.0, 0.0)
        low = stretch * C
        for chunk in range(width // LANES):
            cols = slice(chunk * LANES, (chunk + 1) * LANES)
            padded[chunk, :EDGE] = held[low : low + EDGE, cols] * before
            padded[chunk, EDGE : EDGE + C] = held[low + EDGE : low + EDGE + C, cols]
            padded[chunk, EDGE + C :] = held[low + EDGE + C : low + 2 * EDGE + C, cols] * after
        for chunk in range(width // LANES):
            cols = slice(chunk * LANES, (chunk + 1) * LANES)
            for part in range(0, C, 64):
                total = jnp.zeros((64, LANES), jnp.float32)
                for tap in range(taps_ref.shape[0]):
                    at_row = EDGE - half + part + tap
                    total = total + padded[chunk, at_row : at_row + 64] * taps[tap : tap + 1, cols]
                sum_ref[low + part : low + part + 64, cols] = total


def tail_kernel(
    sum_ref, halo_ref, taps_ref, flags_ref, first_ref, gain_depth_ref, gain_ffn_ref, gain_final_ref,
    w_point_ref, up_own_ref, up_other_ref, down_own_ref, down_other_ref,
    out_ref,
    around, depth, normed, second, hidden, feed,
):
    rows, width = sum_ref.shape
    half = (taps_ref.shape[0] - 1) // 2
    units = up_own_ref.shape[1]
    step = 512
    core = lax.axis_index("mp")
    at = 2 + 3 * core
    same = jnp.where(
        flags_ref[1, pl.ds(at, 1), :] == flags_ref[1, pl.ds(at - 1 + 2 * core, 1), :], 1.0, 0.0
    )
    taps = taps_ref[...].astype(jnp.float32)
    depth[...] = sum_ref[...]
    around[...] = jnp.zeros_like(around)
    for chunk in range(width // LANES):
        cols = slice(chunk * LANES, (chunk + 1) * LANES)
        around[chunk, pl.ds(pl.multiple_of(core * 2 * EDGE, EDGE), EDGE)] = (
            halo_ref[:, cols].astype(jnp.float32) * same
        )
    edge = pl.ds(pl.multiple_of(core * (rows - EDGE), EDGE), EDGE)
    for chunk in range(width // LANES):
        cols = slice(chunk * LANES, (chunk + 1) * LANES)
        total = jnp.zeros((EDGE, LANES), jnp.float32)
        for tap in range(taps_ref.shape[0]):
            at_row = EDGE - half + tap
            total = total + around[chunk, at_row : at_row + EDGE] * taps[tap : tap + 1, cols]
        depth[edge, cols] = depth[edge, cols] + total

    def squash(part):
        value = norm_rows(depth[part], gain_depth_ref[...])
        normed[part] = (value * sigmoid(value)).astype(jnp.bfloat16)

    each(rows, 16, squash)
    second[...] = first_ref[...] + jnp.dot(
        normed[...], w_point_ref[...], preferred_element_type=jnp.float32
    )

    def ffn_norm(part):
        normed[part] = norm_rows(second[part], gain_ffn_ref[...]).astype(jnp.bfloat16)

    each(rows, 16, ffn_norm)
    for group, ref in enumerate((up_own_ref, up_other_ref)):
        for part in range(units // step):
            cols = slice(part * step, (part + 1) * step)
            value = jnp.dot(normed[...], ref[:, cols], preferred_element_type=jnp.float32)
            hidden[group, :, cols] = (value * sigmoid(value)).astype(jnp.bfloat16)
    for part in range(width // 256):
        cols = slice(part * 256, (part + 1) * 256)
        total = 0.0
        for group, ref in enumerate((down_own_ref, down_other_ref)):
            total = total + jnp.dot(
                hidden[group], ref[:, cols], preferred_element_type=jnp.float32
            ).astype(jnp.bfloat16).astype(jnp.float32)
        feed[:, cols] = second[:, cols] + 0.5 * total

    def finish(part):
        out_ref[part] = norm_rows(feed[part], gain_final_ref[...]).astype(jnp.bfloat16)

    each(rows, 16, finish)


def on_device(
    frames,
    gain_attn,
    w_qkv,
    w_out,
    gain_conv,
    w_point_in,
    w_depth,
    gain_depth,
    w_point_out,
    gain_ffn,
    w_up,
    w_down,
    gain_final,
    lengths,
    context,
):
    slab, width = frames.shape
    rows = slab // 2
    local = w_qkv.shape[2]
    window = rows + EDGE
    units = w_up.shape[1]
    tm = lax.axis_size("tm")
    bf16, f32 = jnp.bfloat16, jnp.float32
    shape = jax.ShapeDtypeStruct
    swap = [(0, 1), (1, 0)]

    def row(vec):
        return vec.reshape(1, -1)

    w_planes = jnp.transpose(w_qkv, (1, 0, 2))
    sent, sent_far, normed = pl.pallas_call(
        send_kernel,
        out_shape=(
            shape((rows, width), bf16),
            shape((rows + SPARE, width), bf16),
            shape((slab, width), bf16),
        ),
        in_specs=[HBM] * 2,
        out_specs=(VMEM,) * 3,
        scratch_shapes=[
            pltpu.VMEM((slab, width), bf16),
            pltpu.VMEM((1, width), f32),
            pltpu.SemaphoreType.DMA((3,)),
        ],
        compiler_params=params(8),
        cost_estimate=cost(0, 2 * rows * width * 2),
        name="send_norm",
    )(in_hbm(frames), in_hbm(row(gain_attn)))
    up_held, down_held, sent = lax.optimization_barrier((w_up, w_down, sent))
    up_other = lax.ppermute(up_held, "mp", swap)
    down_other = lax.ppermute(down_held, "mp", swap)
    near_mine = lax.ppermute(sent, "tm", [(i, i + 1) for i in range(tm - 1)])
    far_mine = lax.ppermute(sent_far, "tm", [(i, i + 2) for i in range(tm - 2)])
    qkv, flags = pl.pallas_call(
        own_kernel,
        out_shape=(shape((3, slab, local), bf16), shape((2, 8, LANES), f32)),
        in_specs=[VMEM] + [HBM] * 3,
        out_specs=(VMEM,) * 2,
        scratch_shapes=[
            pltpu.VMEM((3, width, local), bf16),
            pltpu.VMEM((1, lengths.shape[0]), jnp.int32),
            pltpu.VMEM((1, lengths.shape[0]), jnp.int32),
            pltpu.SemaphoreType.DMA((5,)),
        ],
        compiler_params=params(ROOMY),
        cost_estimate=cost(slab * width * 3 * local, width * 3 * local * 2, EARLY),
        name="own_qkv",
    )(normed, in_hbm(w_planes), in_hbm(row(lengths)), in_hbm(row(context)))
    partial = (shape((slab, local), f32),) * 3
    own_parts = pl.pallas_call(
        self_kernel,
        out_shape=partial,
        in_specs=[VMEM] * 2,
        out_specs=(VMEM,) * 3,
        compiler_params=params(16),
        cost_estimate=cost(5 * slab * slab * local, 4 * MIB, EARLY),
        name="own_attention",
    )(qkv, flags)
    near_mine, own_parts = lax.optimization_barrier((near_mine, own_parts))
    near_theirs = lax.ppermute(near_mine, "mp", swap)
    near_parts = own_parts
    for theirs, part in enumerate((near_mine, near_theirs)):
        near_parts = pl.pallas_call(
            functools.partial(near_kernel, bool(theirs)),
            out_shape=partial,
            in_specs=[VMEM] * 7,
            out_specs=(VMEM,) * 3,
            scratch_shapes=[
                pltpu.VMEM((rows, local), bf16),
                pltpu.VMEM((rows, local), bf16),
            ],
            compiler_params=params(16),
            cost_estimate=cost(
                slab * width * local + 4 * slab * slab * local, 8 * MIB, MIDDLE
            ),
            name="near_theirs" if theirs else "near_mine",
        )(qkv, part, w_planes, flags, *near_parts)
    far_mine, near_parts = lax.optimization_barrier((far_mine, near_parts))
    far_theirs = lax.ppermute(far_mine, "mp", swap)
    halves = [pltpu.VMEM((rows, local), bf16)] * 2
    far_parts = pl.pallas_call(
        far_mine_kernel,
        out_shape=partial,
        in_specs=[VMEM] * 7,
        out_specs=(VMEM,) * 3,
        scratch_shapes=halves,
        compiler_params=params(16),
        cost_estimate=cost(slab * width * local + 2 * slab * slab * local, 8 * MIB, MIDDLE),
        name="far_mine",
    )(qkv, far_mine, w_planes, flags, *near_parts)
    heads, to_other = pl.pallas_call(
        far_theirs_kernel,
        out_shape=(shape((slab, local), bf16), shape((window, width), bf16)),
        in_specs=[VMEM] * 8,
        out_specs=(VMEM,) * 2,
        scratch_shapes=halves,
        compiler_params=params(16),
        cost_estimate=cost(slab * width * 2 * local + 3 * slab * slab * local, 10 * MIB, LATE),
        name="far_theirs",
    )(qkv, far_theirs, w_planes, flags, *far_parts, w_out)
    from_other = lax.ppermute(to_other, "mp", swap)
    base = pl.pallas_call(
        base_kernel,
        out_shape=shape((window, width), f32),
        in_specs=[VMEM] * 3,
        out_specs=VMEM,
        compiler_params=params(12),
        cost_estimate=cost(window * width * local, 3 * MIB),
        name="out_projection",
    )(heads, w_out, frames)
    gated, edge, first_res = pl.pallas_call(
        gate_kernel,
        out_shape=(
            shape((window, width), bf16),
            shape((EDGE, width), bf16),
            shape((rows, width), f32),
        ),
        in_specs=[VMEM] * 4,
        out_specs=(VMEM,) * 3,
        scratch_shapes=[pltpu.VMEM((window, width), bf16), pltpu.VMEM((window, width), f32)],
        compiler_params=params(16),
        cost_estimate=cost(window * width * 2 * width, 5 * MIB),
        name="gated_units",
    )(base, from_other, row(gain_conv), w_point_in)
    halo_pairs = [(2 * i + 1, 2 * i + 2) for i in range(tm - 1)]
    halo = lax.ppermute(edge, ("tm", "mp"), halo_pairs + [(b, a) for a, b in halo_pairs])
    depth_sum = pl.pallas_call(
        conv_kernel,
        out_shape=shape((rows, width), f32),
        in_specs=[VMEM] * 3,
        out_specs=VMEM,
        scratch_shapes=[
            pltpu.VMEM((rows + 2 * EDGE, width), f32),
            pltpu.VMEM((width // LANES, C + 2 * EDGE, LANES), f32),
        ],
        compiler_params=params(12),
        cost_estimate=cost(rows * width * 512, MIB),
        name="depthwise",
    )(gated, w_depth, flags)
    return pl.pallas_call(
        tail_kernel,
        out_shape=shape((rows, width), bf16),
        in_specs=[VMEM] * 13,
        out_specs=VMEM,
        scratch_shapes=[
            pltpu.VMEM((width // LANES, 3 * EDGE, LANES), f32),
            pltpu.VMEM((rows, width), f32),
            pltpu.VMEM((rows, width), bf16),
            pltpu.VMEM((rows, width), f32),
            pltpu.VMEM((2, rows, units), bf16),
            pltpu.VMEM((rows, width), f32),
        ],
        compiler_params=params(12),
        cost_estimate=cost(rows * width * 9 * width, 18 * MIB),
        name="tail",
    )(
        depth_sum, halo, w_depth, flags, first_res, row(gain_depth), row(gain_ffn),
        row(gain_final), w_point_out, w_up, up_other, w_down, down_other,
    )


def solution(mesh):
    in_specs = (
        P("tm", None),
        P(),
        P(None, None, "mp"),
        P("mp", None),
        P(),
        P(),
        P(),
        P(),
        P(),
        P(),
        P(None, "mp"),
        P("mp", None),
        P(),
        P(),
        P(),
    )
    out_specs = P(("tm", "mp"), None)
    return jax.shard_map(
        on_device, mesh=mesh, in_specs=in_specs, out_specs=out_specs, check_vma=False
    )
```
